32 devices in a mesh: cells: 8 (over z, x), rhs: 4 (over y, core).
Axes of the slice: x: 2, y: 2, z: 4, core: 2. Of those that a mesh axis runs over, the one named last changes fastest.
Arguments:
- right_side: bfloat16 [64, 512, 384], P('cells', 'rhs'), may hold values from -6 to 6
- leaf_inverse: bfloat16 [64, 384, 384], P('cells'), may hold values from -0.3125 to 0.3125
- leaf_couple: bfloat16 [64, 9, 384, 128], P('cells'), may hold values from -0.3125 to 0.3125
- skel_target: int32 [64, 9], P('cells'), may hold values from 0 to 255, as said below
- skeleton_in: float32 [512, 256, 128], P('rhs', 'cells'), may hold values from -6 to 6
- lift_ops: bfloat16 [8, 4096, 512], P('cells', None, 'rhs'), may hold values from -0.09375 to 0.09375
- node_mix: bfloat16 [8, 1024, 512], P('cells', None, 'rhs'), may hold values from -0.1875 to 0.1875
- node_couple: bfloat16 [8, 512, 512], P('cells', None, 'rhs'), may hold values from -0.125 to 0.125
Outputs:
- leaf_solution: bfloat16 [64, 512, 384], P('cells', 'rhs')
- skeleton_rhs: float32 [512, 256, 128], P('rhs', 'cells')
- node_solution: bfloat16 [8, 512, 512], P('cells', 'rhs')
- node_skeleton: float32 [8, 512, 512], P('cells', 'rhs')
The draws below stay inside these ranges and needn't reach their ends.
Inputs may be any that keep to these rules, and one draw needn't show every extreme that they name: `skel_target`: entry (c, k) names a skeleton block; its owner device, the entry // 32, lies at most 2 positions along cells from the cell's device c // 8, and on every device some slot reaches that distance.
All inputs are finite; a program needn't handle non-finite values.
Results may differ from the reference program's by a relative error of at most 0.03.
Values may be sent and summed in bfloat16 or wider, within the bound.
A program may use at most 128 MiB of HBM per device.

```python
import jax
import jax.numpy as jnp
from jax import lax

SLOTS = 9
HOP = 2
CELLS_DEV = 8
RW = 384
SW = 128
MW = 512
SB = 32
SBW = 4096
NC = 64
NSB = 256
COLS = 512
LEVELS = 3
N_CELLS = 8


def draw_skel_target(key, part):
    key_offset = jax.random.fold_in(key, 11)
    key_block = jax.random.fold_in(key, 23)
    cell_device = (jnp.arange(NC) // CELLS_DEV).astype(jnp.int32)
    offsets = jax.random.randint(key_offset, (NC, SLOTS), -HOP, HOP + 1).astype(jnp.int32)
    first_slot = (jnp.arange(NC) % CELLS_DEV == 0)[:, None] & (jnp.arange(SLOTS) == 0)[None, :]
    farthest = jnp.where(cell_device + HOP < N_CELLS, HOP, -HOP).astype(jnp.int32)
    offsets = jnp.where(first_slot, farthest[:, None], offsets)
    owner_dev = cell_device[:, None] + offsets
    owner_dev = jnp.where(owner_dev < 0, -owner_dev, owner_dev)
    owner_dev = jnp.where(owner_dev > N_CELLS - 1, 2 * (N_CELLS - 1) - owner_dev, owner_dev)
    block_pick = jax.random.randint(key_block, (NC, SLOTS), 0, SB).astype(jnp.int32)
    return (owner_dev * SB + block_pick).astype(jnp.int32)


def level_of(rng, dims, pieces, smallest, high):
    loudness = 1.0
    for axis_at, parts in pieces:
        draws = jax.random.uniform(jax.random.fold_in(jax.random.fold_in(rng, 6), axis_at), (parts,), jnp.float32, smallest / len(pieces), high / len(pieces))
        loudness = loudness * jnp.repeat(jnp.exp(draws), dims[axis_at] // parts).reshape((-1,) + (1,) * (len(dims) - 1 - axis_at))
    return loudness


def gaussian(rng, dims, width, limit, cuts=(), dtype=jnp.bfloat16):
    drawn = width * jax.random.normal(rng, dims, jnp.float32)
    if cuts:
        drawn = drawn * level_of(rng, dims, cuts, -0.22, 0.18)
    return jnp.clip(drawn, -limit, limit).astype(dtype)


def setup_inputs(seed: int = 0) -> dict:
    streams_of = jax.random.split(jax.random.key(seed), 9)
    return {
        "right_side": gaussian(streams_of[0], (NC, COLS, RW), 1.0, 6.0, ((0, 8), (1, 4))),
        "leaf_inverse": gaussian(streams_of[1], (NC, RW, RW), RW ** -0.5, 0.3125, ((0, 8),)),
        "leaf_couple": gaussian(streams_of[2], (NC, SLOTS, RW, SW), RW ** -0.5, 0.3125, ((0, 8),)),
        "skel_target": draw_skel_target(jax.random.fold_in(streams_of[8], 71), 0),
        "skeleton_in": gaussian(streams_of[4], (COLS, NSB, SW), 1.0, 6.0, ((0, 4), (1, 8)), jnp.float32),
        "lift_ops": gaussian(streams_of[5], (N_CELLS, SBW, MW), SBW ** -0.5, 0.09375, ((0, 8), (2, 4))),
        "node_mix": gaussian(streams_of[6], (N_CELLS, 2 * MW, MW), (2 * MW) ** -0.5, 0.1875, ((0, 8), (2, 4))),
        "node_couple": gaussian(streams_of[7], (N_CELLS, MW, MW), (4 * MW) ** -0.5, 0.125, ((0, 8), (2, 4))),
    }


def leaf_step(operands):
    rhs_cell, inverse_cell, couple_cell = operands
    solved = jnp.dot(rhs_cell, inverse_cell, preferred_element_type=jnp.float32).astype(jnp.bfloat16)
    updates = jnp.einsum("cr,krs->kcs", solved.astype(jnp.float32), couple_cell.astype(jnp.float32))
    return solved, updates


def lift_step(operands):
    flattened, lift_cell = operands
    return jnp.dot(flattened, lift_cell, preferred_element_type=jnp.float32).astype(jnp.bfloat16)


def combine(left_child, right_child, mix_ops, couple_ops):
    joined = jnp.concatenate([left_child, right_child], axis=-1)
    solution = jnp.einsum("ncw,nwm->ncm", joined.astype(jnp.float32), mix_ops.astype(jnp.float32)).astype(jnp.bfloat16)
    coupled = jnp.einsum("ncw,nwm->ncm", solution.astype(jnp.float32), couple_ops.astype(jnp.float32))
    skeleton = 0.5 * (left_child.astype(jnp.float32) + right_child.astype(jnp.float32)) - coupled
    return solution, skeleton


def reference(right_side, leaf_inverse, leaf_couple, skel_target, skeleton_in, lift_ops, node_mix, node_couple):
    solved, updates = lax.map(leaf_step, (right_side, leaf_inverse, leaf_couple))
    summed = jax.ops.segment_sum(updates.reshape(NC * SLOTS, COLS, SW), skel_target.reshape(NC * SLOTS), num_segments=NSB)
    skeleton_rhs = skeleton_in - jnp.transpose(summed, (1, 0, 2))
    flattened = jnp.transpose(skeleton_rhs.reshape(COLS, N_CELLS, SBW), (1, 0, 2)).astype(jnp.bfloat16)
    carried = lax.map(lift_step, (flattened, lift_ops))
    level_solution = jnp.zeros((N_CELLS, COLS, MW), jnp.bfloat16)
    for section_level in range(1, LEVELS + 1):
        if section_level == 1:
            left_child = jnp.roll(carried, 1, axis=0)
            right_child = carried
        else:
            distance = 2 ** (section_level - 2)
            left_child = jnp.roll(carried, distance, axis=0)
            right_child = jnp.roll(carried, -distance, axis=0)
        level_solution, skeleton = combine(left_child, right_child, node_mix, node_couple)
        carried = skeleton.astype(jnp.bfloat16)
    middle = N_CELLS // 2
    node_solution, node_skeleton = combine(jnp.roll(carried, -middle, axis=0), jnp.roll(level_solution, -middle, axis=0), node_mix, node_couple)
    return solved, skeleton_rhs, node_solution, node_skeleton
```

```python
import functools

import jax
import jax.numpy as jnp
from jax import lax
from jax.experimental import pallas as pl
from jax.experimental.pallas import tpu as pltpu
from jax.sharding import PartitionSpec as P

HOP = 2
DISTANCES = (-2, -1, 1, 2)
CHUNKS = 4
MESH = pl.DeviceIdType.MESH
F32, BF16 = jnp.float32, jnp.bfloat16


def dot(a, b):
    return jnp.dot(a, b, preferred_element_type=F32)


def leaf_kernel(blocks, slots, seg_ref, x_ref, inv_ref, couple_ref, sol_ref, own_ref, send_ref, acc):
    cell = pl.program_id(0)

    @pl.when(cell == 0)
    def _():
        @pl.loop(0, acc.shape[0])
        def _(i):
            acc[i] = jnp.zeros(acc.shape[1:], F32)

    solved = dot(x_ref[0], inv_ref[0]).astype(BF16)
    sol_ref[0] = solved
    width = couple_ref.shape[-1]
    for k in range(0, slots, 2):
        pair = [j for j in (k, k + 1) if j < slots]
        wide = jnp.concatenate([couple_ref[0, j] for j in pair], axis=1)
        update = dot(solved, wide)
        for at, j in enumerate(pair):
            where = seg_ref[cell * slots + j]
            acc[where] += update[:, at * width : (at + 1) * width]

    @pl.when(cell == pl.num_programs(0) - 1)
    def _():
        for row in range(2 * HOP + 1):
            if row == HOP:
                @pl.loop(0, blocks)
                def _(b):
                    own_ref[b] = acc[row * blocks + b]
            else:
                slot = row if row < HOP else row - 1

                @pl.loop(0, blocks)
                def _(b):
                    send_ref[slot, b] = acc[row * blocks + b].astype(BF16)


def leaf_call(segments, right_side, leaf_inverse, leaf_couple, blocks):
    cells, columns, rw = right_side.shape
    slots, width = leaf_couple.shape[1], leaf_couple.shape[3]
    grid_spec = pltpu.PrefetchScalarGridSpec(
        num_scalar_prefetch=1,
        grid=(cells,),
        in_specs=[
            pl.BlockSpec((1, columns, rw), lambda c, s: (c, 0, 0)),
            pl.BlockSpec((1, rw, rw), lambda c, s: (c, 0, 0)),
            pl.BlockSpec((1, slots, rw, width), lambda c, s: (c, 0, 0, 0)),
        ],
        out_specs=[
            pl.BlockSpec((1, columns, rw), lambda c, s: (c, 0, 0)),
            pl.BlockSpec((blocks, columns, width), lambda c, s: (0, 0, 0)),
            pl.BlockSpec((2 * HOP, blocks, columns, width), lambda c, s: (0, 0, 0, 0)),
        ],
        scratch_shapes=[pltpu.VMEM(((2 * HOP + 1) * blocks, columns, width), F32)],
    )
    return pl.pallas_call(
        functools.partial(leaf_kernel, blocks, slots),
        grid_spec=grid_spec,
        out_shape=[
            jax.ShapeDtypeStruct((cells, columns, rw), BF16),
            jax.ShapeDtypeStruct((blocks, columns, width), F32),
            jax.ShapeDtypeStruct((2 * HOP, blocks, columns, width), BF16),
        ],
        compiler_params=pltpu.CompilerParams(vmem_limit_bytes=48 * 2**20),
    )(segments, right_side, leaf_inverse, leaf_couple)


def tree_kernel(
    n, levels, send, own, skel, lift, mix, couple, out_skel, out_sol, out_node,
    recv, own_v, skel_v, flat, lift_g, mix_g, couple_g, mine, left_v, right_v, sol_v,
    local_sem, port_send, port_recv, near_send, near_recv, far_send, far_recv, fwd_send, fwd_recv,
    vec_send, vec_recv,
):
    me = lax.axis_index("cells")
    rank = lax.axis_index("rhs")
    near = rank + 1 - 2 * (rank % 2)
    far = (rank + 2) % 4
    far_near = (near + 2) % 4
    blocks, columns, width = own_v.shape
    node = couple_g.shape[0]
    reach = [max(1, 2 ** (level - 2)) for level in range(1, levels + 1)]
    partners = sorted({s % n for d in reach + [1, 2, n // 2] for s in (d, -d)})

    barrier = pltpu.get_barrier_semaphore()
    for step in partners:
        pl.semaphore_signal(barrier, inc=1, device_id=((me + step) % n, rank), device_id_type=MESH)
    for other in (near, far):
        pl.semaphore_signal(barrier, inc=1, device_id=(me, other), device_id_type=MESH)
    pl.semaphore_wait(barrier, len(partners) + 2)

    def shard(which):
        return pl.ds(pl.multiple_of(which * width, width), width)

    def remote(src, dst, s_sem, r_sem, cell, at):
        return pltpu.make_async_remote_copy(
            src_ref=src, dst_ref=dst, send_sem=s_sem, recv_sem=r_sem,
            device_id=(cell, at), device_id_type=MESH,
        )

    group = blocks // CHUNKS
    depth = lift.shape[0] // CHUNKS
    pieces = [(lift, lift_g, pl.ds(q * depth, depth)) for q in range(CHUNKS)]
    pieces += [(mix, mix_g, pl.ds(0, mix.shape[0])), (couple, couple_g, pl.ds(0, couple.shape[0]))]

    def to_near(i):
        src, dst, rows = pieces[i]
        return remote(src.at[rows], dst.at[rows, shard(rank)], near_send.at[i], near_recv.at[i], me, near)

    def to_far(i):
        src, dst, rows = pieces[i]
        return remote(src.at[rows], dst.at[rows, shard(rank)], far_send.at[i], far_recv.at[i], me, far)

    def forward(i):
        _, dst, rows = pieces[i]
        place = dst.at[rows, shard(far)]
        return remote(place, place, fwd_send.at[i], fwd_recv.at[i], me, near)

    def near_arrival(i):
        _, dst, rows = pieces[i]
        place = dst.at[rows, shard(near)]
        return remote(place, place, near_send.at[i], near_recv.at[i], me, near)

    def far_arrival(i):
        _, dst, rows = pieces[i]
        place = dst.at[rows, shard(far)]
        return remote(place, place, far_send.at[i], far_recv.at[i], me, far)

    def fwd_arrival(i):
        _, dst, rows = pieces[i]
        place = dst.at[rows, shard(far_near)]
        return remote(place, place, fwd_send.at[i], fwd_recv.at[i], me, near)

    def portion(j, q):
        rows = pl.ds(q * group, group)
        return remote(
            send.at[j, rows], recv.at[j, rows], port_send.at[j, q], port_recv.at[j, q],
            (me + DISTANCES[j] + n) % n, rank,
        )

    def sends_to(j):
        target = me + DISTANCES[j]
        return jnp.logical_and(target >= 0, target < n)

    def hears_from(j):
        source = me - DISTANCES[j]
        return jnp.logical_and(source >= 0, source < n)

    to_far(0).start()
    for q in range(CHUNKS):
        for j in range(len(DISTANCES)):
            @pl.when(sends_to(j))
            def _():
                portion(j, q).start()
        if q == 0:
            for i in range(1, len(pieces)):
                to_far(i).start()
    for i in range(len(pieces)):
        to_near(i).start()
    locals_ = [
        pltpu.make_async_copy(own, own_v, local_sem.at[0]),
        pltpu.make_async_copy(skel, skel_v, local_sem.at[1]),
    ]
    for i, (src, dst, rows) in enumerate(pieces):
        locals_.append(pltpu.make_async_copy(src.at[rows], dst.at[rows, shard(rank)], local_sem.at[2 + i]))
    for copy in locals_:
        copy.start()

    for j in range(len(DISTANCES)):
        @pl.when(jnp.logical_not(hears_from(j)))
        def _():
            @pl.loop(0, blocks)
            def _(b):
                recv[j, b] = jnp.zeros((columns, width), BF16)

    for copy in locals_:
        copy.wait()

    total = None
    for q in range(CHUNKS):
        ready = [q] if q < CHUNKS - 1 else list(range(q, len(pieces)))
        for i in ready:
            far_arrival(i).wait_recv()
            forward(i).start()
        for j in range(len(DISTANCES)):
            @pl.when(hears_from(j))
            def _():
                portion(j, q).wait_recv()
        for b in range(q * group, (q + 1) * group):
            rows = pl.ds(b, columns, stride=blocks)
            arrived = own_v[b]
            for j in range(len(DISTANCES)):
                arrived = arrived + recv[j, b].astype(F32)
            value = skel_v[rows, :] - arrived
            skel_v[rows, :] = value
            flat[:, b * width : (b + 1) * width] = value.astype(BF16)
        near_arrival(q).wait_recv()
        fwd_arrival(q).wait_recv()
        part = dot(flat[:, q * depth : (q + 1) * depth], lift_g[q * depth : (q + 1) * depth, :])
        total = part if total is None else total + part
    mine[0] = total.astype(BF16)

    def vector(src, dst, at, step):
        return remote(src, dst, vec_send.at[at], vec_recv.at[at], (me + step + n) % n, rank)

    result = pltpu.make_async_copy(skel_v, out_skel, local_sem.at[0])
    sent = []

    def merge(first, second):
        solved = (dot(first, mix_g[:node, :]) + dot(second, mix_g[node:, :])).astype(BF16)
        skeleton = 0.5 * (first.astype(F32) + second.astype(F32)) - dot(solved, couple_g[...])
        return solved, skeleton

    solved = None
    for level in range(levels):
        d = reach[level]
        up = vector(mine.at[level], left_v.at[level], 2 * level, d)
        up.start()
        sent.append(up)
        if level > 0:
            down = vector(mine.at[level], right_v.at[level], 2 * level + 1, -d)
            down.start()
            sent.append(down)
        else:
            result.start()
            for i in range(CHUNKS, len(pieces)):
                near_arrival(i).wait_recv()
                fwd_arrival(i).wait_recv()
        up.wait_recv()
        if level > 0:
            down.wait_recv()
            second = right_v[level]
        else:
            second = mine[0]
        solved, skeleton = merge(left_v[level], second)
        if level == levels - 1:
            sol_v[...] = solved
            other = vector(sol_v, right_v.at[0], 2 * levels, n // 2)
            other.start()
        mine[level + 1] = skeleton.astype(BF16)
    up = vector(mine.at[levels], left_v.at[levels], 2 * levels + 1, n // 2)
    up.start()
    sent += [other, up]
    other.wait_recv()
    up.wait_recv()
    solved, skeleton = merge(left_v[levels], right_v[0])
    out_sol[...] = solved
    out_node[...] = skeleton

    for copy in sent:
        copy.wait_send()
    for i in range(len(pieces)):
        to_near(i).wait_send()
        to_far(i).wait_send()
        forward(i).wait_send()
    for j in range(len(DISTANCES)):
        @pl.when(sends_to(j))
        def _():
            for q in range(CHUNKS):
                portion(j, q).wait_send()
    result.wait()


def tree_call(n, send, own, skel, lift, mix, couple):
    blocks, columns, width = own.shape
    node = couple.shape[0]
    levels = n.bit_length() - 1
    pieces = CHUNKS + 2
    dma = pltpu.SemaphoreType.DMA
    vmem = pl.BlockSpec(memory_space=pltpu.VMEM)
    hbm = pl.BlockSpec(memory_space=pl.ANY)
    return pl.pallas_call(
        functools.partial(tree_kernel, n, levels),
        out_shape=[
            jax.ShapeDtypeStruct(skel.shape, F32),
            jax.ShapeDtypeStruct((columns, node), BF16),
            jax.ShapeDtypeStruct((columns, node), F32),
        ],
        in_specs=[hbm] * 6,
        out_specs=[hbm, vmem, vmem],
        scratch_shapes=[
            pltpu.VMEM((2 * HOP, blocks, columns, width), BF16),
            pltpu.VMEM((blocks, columns, width), F32),
            pltpu.VMEM(skel.shape, F32),
            pltpu.VMEM((columns, blocks * width), BF16),
            pltpu.VMEM((lift.shape[0], node), BF16),
            pltpu.VMEM((mix.shape[0], node), BF16),
            pltpu.VMEM((couple.shape[0], node), BF16),
            pltpu.VMEM((levels + 1, columns, node), BF16),
            pltpu.VMEM((levels + 1, columns, node), BF16),
            pltpu.VMEM((levels, columns, node), BF16),
            pltpu.VMEM((columns, node), BF16),
            dma((2 + pieces,)),
            dma((2 * HOP, CHUNKS)),
            dma((2 * HOP, CHUNKS)),
            dma((pieces,)), dma((pieces,)), dma((pieces,)),
            dma((pieces,)), dma((pieces,)), dma((pieces,)),
            dma((2 * levels + 2,)),
            dma((2 * levels + 2,)),
        ],
        compiler_params=pltpu.CompilerParams(
            collective_id=0, has_side_effects=True, vmem_limit_bytes=48 * 2**20
        ),
    )(send, own, skel, lift, mix, couple)


def on_device(
    right_side, leaf_inverse, leaf_couple, skel_target, skeleton_in, lift_ops, node_mix, node_couple
):
    position = lax.axis_index("cells")
    n = lax.axis_size("cells")
    columns, blocks, width = skeleton_in.shape
    segments = skel_target.reshape(-1) - (position - HOP) * blocks
    solved, own, send = leaf_call(segments, right_side, leaf_inverse, leaf_couple, blocks)
    skel, node_solution, node_skeleton = tree_call(
        n, send, own, skeleton_in.reshape(columns * blocks, width),
        lift_ops[0], node_mix[0], node_couple[0],
    )
    return (
        solved,
        skel.reshape(columns, blocks, width),
        node_solution[None],
        node_skeleton[None],
    )


def solution(mesh):
    return jax.shard_map(
        on_device,
        mesh=mesh,
        in_specs=(
            P("cells", "rhs", None),
            P("cells", None, None),
            P("cells", None, None, None),
            P("cells", None),
            P("rhs", "cells", None),
            P("cells", None, "rhs"),
            P("cells", None, "rhs"),
            P("cells", None, "rhs"),
        ),
        out_specs=(
            P("cells", "rhs", None),
            P("rhs", "cells", None),
            P("cells", "rhs", None),
            P("cells", "rhs", None),
        ),
        check_vma=False,
    )
```

```python
import functools

import jax
import jax.numpy as jnp
from jax import lax
from jax.experimental import pallas as pl
from jax.experimental.pallas import tpu as pltpu
from jax.sharding import PartitionSpec as P

HOP = 2
CHUNKS = 4
MESH = pl.DeviceIdType.MESH
F32, BF16 = jnp.float32, jnp.bfloat16


def dot(a, b):
    return jnp.dot(a, b, preferred_element_type=F32)


def leaf_kernel(blocks, slots, seg_ref, x_ref, inv_ref, couple_ref, sol_ref, own_ref, send_ref, acc):
    cell = pl.program_id(0)

    @pl.when(cell == 0)
    def _():
        @pl.loop(0, acc.shape[0])
        def _(i):
            acc[i] = jnp.zeros(acc.shape[1:], F32)

    solved = dot(x_ref[0], inv_ref[0]).astype(BF16)
    sol_ref[0] = solved
    width = couple_ref.shape[-1]
    for k in range(0, slots, 2):
        pair = [j for j in (k, k + 1) if j < slots]
        wide = jnp.concatenate([couple_ref[0, j] for j in pair], axis=1)
        update = dot(solved, wide)
        for at, j in enumerate(pair):
            where = seg_ref[cell * slots + j]
            acc[where] += update[:, at * width : (at + 1) * width]

    @pl.when(cell == pl.num_programs(0) - 1)
    def _():
        for row in range(2 * HOP + 1):
            if row == HOP:
                @pl.loop(0, blocks)
                def _(b):
                    own_ref[b] = acc[row * blocks + b]
            else:
                slot = row if row < HOP else row - 1

                @pl.loop(0, blocks)
                def _(b):
                    send_ref[slot, b] = acc[row * blocks + b].astype(BF16)


def leaf_call(segments, right_side, leaf_inverse, leaf_couple, blocks):
    cells, columns, rw = right_side.shape
    slots, width = leaf_couple.shape[1], leaf_couple.shape[3]
    grid_spec = pltpu.PrefetchScalarGridSpec(
        num_scalar_prefetch=1,
        grid=(cells,),
        in_specs=[
            pl.BlockSpec((1, columns, rw), lambda c, s: (c, 0, 0)),
            pl.BlockSpec((1, rw, rw), lambda c, s: (c, 0, 0)),
            pl.BlockSpec((1, slots, rw, width), lambda c, s: (c, 0, 0, 0)),
        ],
        out_specs=[
            pl.BlockSpec((1, columns, rw), lambda c, s: (c, 0, 0)),
            pl.BlockSpec((blocks, columns, width), lambda c, s: (0, 0, 0)),
            pl.BlockSpec((2 * HOP, blocks, columns, width), lambda c, s: (0, 0, 0, 0)),
        ],
        scratch_shapes=[pltpu.VMEM(((2 * HOP + 1) * blocks, columns, width), F32)],
    )
    return pl.pallas_call(
        functools.partial(leaf_kernel, blocks, slots),
        grid_spec=grid_spec,
        out_shape=[
            jax.ShapeDtypeStruct((cells, columns, rw), BF16),
            jax.ShapeDtypeStruct((blocks, columns, width), F32),
            jax.ShapeDtypeStruct((2 * HOP, blocks, columns, width), BF16),
        ],
        compiler_params=pltpu.CompilerParams(vmem_limit_bytes=60 * 2**20),
    )(segments, right_side, leaf_inverse, leaf_couple)


def tree_kernel(
    n, levels, send, own, skel, lift, mix, couple, out_skel, out_sol, out_node,
    recv, relay, addend, own_v, skel_v, flat, lift_g, mix_g, couple_g, mix_h, couple_h,
    mine, left_v, right_v,
    local_sem, port_send, port_recv, near_send, near_recv, far_send, far_recv, fwd_send, fwd_recv,
    half_send, half_recv, vec_send, vec_recv,
):
    me = lax.axis_index("cells")
    rank = lax.axis_index("rhs")
    near = rank + 1 - 2 * (rank % 2)
    far = (rank + 2) % 4
    far_near = (near + 2) % 4
    blocks, columns, width = own_v.shape
    node = couple_g.shape[0]
    reach = [max(1, 2 ** (level - 2)) for level in range(1, levels + 1)]
    partners = sorted({s % n for d in reach + [1, 2, n // 2] for s in (d, -d)})
    odd = me % 2
    side = 2 * odd - 1
    diag_slot, beside_slot, ahead_slot, behind_slot = 1 + odd, 2 - odd, 3 * odd, 3 - 3 * odd
    beside = me - side
    ahead, behind = me + 2 * side, me - 2 * side
    has_ahead = jnp.logical_and(ahead >= 0, ahead < n)
    has_behind = jnp.logical_and(behind >= 0, behind < n)
    ahead, behind = (ahead + n) % n, (behind + n) % n

    barrier = pltpu.get_barrier_semaphore()
    for step in partners:
        pl.semaphore_signal(barrier, inc=1, device_id=((me + step) % n, rank), device_id_type=MESH)
    for other in (near, far):
        pl.semaphore_signal(barrier, inc=1, device_id=(me, other), device_id_type=MESH)
    pl.semaphore_wait(barrier, len(partners) + 2)

    def shard(which):
        return pl.ds(pl.multiple_of(which * width, width), width)

    def remote(src, dst, s_sem, r_sem, cell, at):
        return pltpu.make_async_remote_copy(
            src_ref=src, dst_ref=dst, send_sem=s_sem, recv_sem=r_sem,
            device_id=(cell, at), device_id_type=MESH,
        )

    group = blocks // CHUNKS
    depth = lift.shape[0] // CHUNKS
    pieces = [(lift, lift_g, pl.ds(q * depth, depth)) for q in range(CHUNKS)]
    pieces += [(mix, mix_g, pl.ds(0, mix.shape[0])), (couple, couple_g, pl.ds(0, node))]
    count = len(pieces)
    halves = [(mix, mix_h, pl.ds(0, node)), (mix, mix_h, pl.ds(node, node)), (couple, couple_h, pl.ds(0, node))]

    def place(i, which):
        _, dst, rows = (pieces + halves)[i]
        return dst.at[rows, shard(which)]

    def source(i):
        return pieces[i][0].at[pieces[i][2]] if i < count else place(i, rank)

    def to_near(i):
        return remote(source(i), place(i, rank), near_send.at[i], near_recv.at[i], me, near)

    def to_far(i):
        return remote(source(i), place(i, rank), far_send.at[i], far_recv.at[i], me, far)

    def forward(i):
        return remote(place(i, far), place(i, far), fwd_send.at[i], fwd_recv.at[i], me, near)

    def near_arrival(i):
        return remote(place(i, near), place(i, near), near_send.at[i], near_recv.at[i], me, near)

    def far_arrival(i):
        return remote(place(i, far), place(i, far), far_send.at[i], far_recv.at[i], me, far)

    def fwd_arrival(i):
        return remote(place(i, far_near), place(i, far_near), fwd_send.at[i], fwd_recv.at[i], me, near)

    def across(i):
        src, dst, rows = halves[i]
        return remote(
            src.at[rows], dst.at[rows, shard(rank)], half_send.at[i], half_recv.at[i],
            (me + n // 2) % n, rank,
        )

    first_half = CHUNKS // 2

    def rows_of(q):
        return pl.ds(q * group, group)

    def rows_in_half(q):
        return pl.ds((q % first_half) * group, group)

    def diag(q):
        at = 0 if q < first_half else 1
        return remote(
            send.at[diag_slot, rows_of(q)], relay.at[at, rows_in_half(q)],
            port_send.at[0, q], port_recv.at[0, q], beside if at == 0 else ahead, rank,
        )

    def to_beside(q):
        src = send.at[beside_slot, rows_of(q)] if q < first_half else addend.at[1, rows_in_half(q)]
        return remote(src, recv.at[0, rows_of(q)], port_send.at[1, q], port_recv.at[1, q], beside, rank)

    def to_ahead(q):
        return remote(
            send.at[ahead_slot, rows_of(q)], recv.at[1, rows_of(q)],
            port_send.at[2, q], port_recv.at[2, q], ahead, rank,
        )

    def to_behind(q):
        src = send.at[behind_slot, rows_of(q)] if q >= first_half else addend.at[0, rows_in_half(q)]
        return remote(src, recv.at[2, rows_of(q)], port_send.at[3, q], port_recv.at[3, q], behind, rank)

    addends = [
        pltpu.make_async_copy(send.at[behind_slot, pl.ds(0, blocks // 2)], addend.at[0], local_sem.at[0]),
        pltpu.make_async_copy(send.at[beside_slot, pl.ds(blocks // 2, blocks // 2)], addend.at[1], local_sem.at[1]),
    ]
    for at in range(first_half):
        @pl.when(has_ahead)
        def _():
            diag(at).start()
            diag(at + first_half).start()

        @pl.when(has_behind)
        def _():
            to_behind(at + first_half).start()

        to_far(at).start()
    for copy in addends:
        copy.start()
    for at in range(first_half):
        to_beside(at).start()

        @pl.when(has_ahead)
        def _():
            to_ahead(at).start()

        to_far(at + first_half).start()
    for i in range(CHUNKS, count):
        to_far(i).start()

    @pl.when(has_ahead)
    def _():
        for q in range(first_half, CHUNKS):
            to_ahead(q).start()

    for i in range(count):
        to_near(i).start()
    locals_ = [
        pltpu.make_async_copy(own, own_v, local_sem.at[2]),
        pltpu.make_async_copy(skel, skel_v, local_sem.at[3]),
    ]
    for i, (src, dst, rows) in enumerate(pieces):
        locals_.append(pltpu.make_async_copy(src.at[rows], dst.at[rows, shard(rank)], local_sem.at[4 + i]))
    for copy in locals_:
        copy.start()

    for slot, there in ((1, has_behind), (2, has_ahead)):
        @pl.when(jnp.logical_not(there))
        def _():
            @pl.loop(0, blocks)
            def _(b):
                recv[slot, b] = jnp.zeros((columns, width), BF16)

    for copy in locals_:
        copy.wait()
    for b in range(blocks):
        own_v[b] = skel_v[pl.ds(b, columns, stride=blocks), :] - own_v[b]
    for copy in addends:
        copy.wait()

    for at in range(2):
        for q in range(at * first_half, (at + 1) * first_half):
            @pl.when(has_behind)
            def _():
                diag(q).wait_recv()

                @pl.loop((q % first_half) * group, (q % first_half + 1) * group)
                def _(b):
                    addend[at, b] = (addend[at, b].astype(F32) + relay[at, b].astype(F32)).astype(BF16)

                if at == 0:
                    to_behind(q).start()

            if at == 1:
                to_beside(q).start()
        far_arrival(at).wait_recv()
        forward(at).start()

    total = None
    for q in range(CHUNKS):
        for i in ([], [2], [3], list(range(CHUNKS, count)))[q]:
            far_arrival(i).wait_recv()
            forward(i).start()
        to_beside(q).wait_recv()

        @pl.when(has_behind)
        def _():
            to_ahead(q).wait_recv()

        @pl.when(has_ahead)
        def _():
            to_behind(q).wait_recv()

        if q == CHUNKS - 1:
            for i in range(len(halves)):
                across(i).start()
        for b in range(q * group, (q + 1) * group):
            arrived = recv[0, b].astype(F32) + recv[1, b].astype(F32) + recv[2, b].astype(F32)
            value = own_v[b] - arrived
            skel_v[pl.ds(b, columns, stride=blocks), :] = value
            flat[:, b * width : (b + 1) * width] = value.astype(BF16)
        near_arrival(q).wait_recv()
        fwd_arrival(q).wait_recv()
        part = dot(flat[:, q * depth : (q + 1) * depth], lift_g[q * depth : (q + 1) * depth, :])
        total = part if total is None else total + part
    mine[0] = total.astype(BF16)

    def vector(src, dst, at, step):
        return remote(src, dst, vec_send.at[at], vec_recv.at[at], (me + step + n) % n, rank)

    result = pltpu.make_async_copy(skel_v, out_skel, local_sem.at[0])
    sent = []

    def merge(first, second, mixing, coupling):
        solved = (dot(first, mixing[:node, :]) + dot(second, mixing[node:, :])).astype(BF16)
        skeleton = 0.5 * (first.astype(F32) + second.astype(F32)) - dot(solved, coupling[...])
        return solved, skeleton

    def pass_on(i):
        across(i).wait_recv()
        to_far(count + i).start()
        to_near(count + i).start()

    for level in range(levels - 1):
        d = reach[level]
        up = vector(mine.at[level], left_v.at[level], 2 * level, d)
        up.start()
        sent.append(up)
        if level > 0:
            down = vector(mine.at[level], right_v.at[level], 2 * level + 1, -d)
            down.start()
            sent.append(down)
        else:
            result.start()
            for i in range(CHUNKS, count):
                near_arrival(i).wait_recv()
                fwd_arrival(i).wait_recv()
        up.wait_recv()
        if level > 0:
            down.wait_recv()
            second = right_v[level]
        else:
            second = mine[0]
        _, skeleton = merge(left_v[level], second, mix_g, couple_g)
        mine[level + 1] = skeleton.astype(BF16)

    last = levels - 1
    up = vector(mine.at[last], left_v.at[last], 2 * last, reach[last])
    down = vector(mine.at[last], right_v.at[last], 2 * last + 1, -reach[last])
    up.start()
    down.start()
    sent += [up, down]
    for i in range(len(halves)):
        pass_on(i)
    for i in range(count, count + len(halves)):
        far_arrival(i).wait_recv()
        forward(i).start()
    up.wait_recv()
    down.wait_recv()
    for i in range(count, count + len(halves)):
        near_arrival(i).wait_recv()
        fwd_arrival(i).wait_recv()
    solved, skeleton = merge(right_v[last], left_v[last], mix_h, couple_h)
    solved, skeleton = merge(skeleton.astype(BF16), solved, mix_g, couple_g)
    out_sol[...] = solved
    out_node[...] = skeleton

    for copy in sent:
        copy.wait_send()
    for i in range(count + len(halves)):
        to_near(i).wait_send()
        to_far(i).wait_send()
        forward(i).wait_send()
    for i in range(len(halves)):
        across(i).wait_send()
    for q in range(CHUNKS):
        to_beside(q).wait_send()

        @pl.when(has_ahead)
        def _():
            diag(q).wait_send()
            to_ahead(q).wait_send()

        @pl.when(has_behind)
        def _():
            to_behind(q).wait_send()

    result.wait()


def tree_call(n, send, own, skel, lift, mix, couple):
    blocks, columns, width = own.shape
    node = couple.shape[0]
    levels = n.bit_length() - 1
    pieces = CHUNKS + 2 + 3
    dma = pltpu.SemaphoreType.DMA
    vmem = pl.BlockSpec(memory_space=pltpu.VMEM)
    hbm = pl.BlockSpec(memory_space=pl.ANY)
    return pl.pallas_call(
        functools.partial(tree_kernel, n, levels),
        out_shape=[
            jax.ShapeDtypeStruct(skel.shape, F32),
            jax.ShapeDtypeStruct((columns, node), BF16),
            jax.ShapeDtypeStruct((columns, node), F32),
        ],
        in_specs=[hbm] * 6,
        out_specs=[hbm, vmem, vmem],
        scratch_shapes=[
            pltpu.VMEM((3, blocks, columns, width), BF16),
            pltpu.VMEM((2, blocks // 2, columns, width), BF16),
            pltpu.VMEM((2, blocks // 2, columns, width), BF16),
            pltpu.VMEM((blocks, columns, width), F32),
            pltpu.VMEM(skel.shape, F32),
            pltpu.VMEM((columns, blocks * width), BF16),
            pltpu.VMEM((lift.shape[0], node), BF16),
            pltpu.VMEM((mix.shape[0], node), BF16),
            pltpu.VMEM((couple.shape[0], node), BF16),
            pltpu.VMEM((mix.shape[0], node), BF16),
            pltpu.VMEM((couple.shape[0], node), BF16),
            pltpu.VMEM((levels, columns, node), BF16),
            pltpu.VMEM((levels, columns, node), BF16),
            pltpu.VMEM((levels, columns, node), BF16),
            dma((4 + CHUNKS + 2,)),
            dma((4, CHUNKS)),
            dma((4, CHUNKS)),
            dma((pieces,)), dma((pieces,)), dma((pieces,)),
            dma((pieces,)), dma((pieces,)), dma((pieces,)),
            dma((3,)), dma((3,)),
            dma((2 * levels,)),
            dma((2 * levels,)),
        ],
        compiler_params=pltpu.CompilerParams(
            collective_id=0, has_side_effects=True, vmem_limit_bytes=60 * 2**20
        ),
    )(send, own, skel, lift, mix, couple)


def on_device(
    right_side, leaf_inverse, leaf_couple, skel_target, skeleton_in, lift_ops, node_mix, node_couple
):
    position = lax.axis_index("cells")
    n = lax.axis_size("cells")
    columns, blocks, width = skeleton_in.shape
    segments = skel_target.reshape(-1) - (position - HOP) * blocks
    solved, own, send = leaf_call(segments, right_side, leaf_inverse, leaf_couple, blocks)
    skel, node_solution, node_skeleton = tree_call(
        n, send, own, skeleton_in.reshape(columns * blocks, width),
        lift_ops[0], node_mix[0], node_couple[0],
    )
    return (
        solved,
        skel.reshape(columns, blocks, width),
        node_solution[None],
        node_skeleton[None],
    )


def solution(mesh):
    return jax.shard_map(
        on_device,
        mesh=mesh,
        in_specs=(
            P("cells", "rhs", None),
            P("cells", None, None),
            P("cells", None, None, None),
            P("cells", None),
            P("rhs", "cells", None),
            P("cells", None, "rhs"),
            P("cells", None, "rhs"),
            P("cells", None, "rhs"),
        ),
        out_specs=(
            P("cells", "rhs", None),
            P("rhs", "cells", None),
            P("cells", "rhs", None),
            P("cells", "rhs", None),
        ),
        check_vma=False,
    )
```

```python
import functools

import jax
import jax.numpy as jnp
from jax import lax
from jax.experimental import pallas as pl
from jax.experimental.pallas import tpu as pltpu
from jax.sharding import PartitionSpec as P

HOP = 2
CHUNKS = 4
MESH = pl.DeviceIdType.MESH
F32, BF16 = jnp.float32, jnp.bfloat16


def dot(a, b):
    return jnp.dot(a, b, preferred_element_type=F32)


def tree_kernel(
    n, levels, prev, last_of, rhs, inverse, leaf_couple, skel, lift, mix, couple,
    out_leaf, out_skel, out_sol, out_node,
    rhs_v, inverse_v, leaf_couple_v, leaf_v, partial, send, recv, relay, own_v, skel_v, flat, lift_g, mix_g, couple_g, mix_h, couple_h,
    mine, left_v, right_v,
    leaf_sem, local_sem, port_send, port_recv, near_send, near_recv, far_send, far_recv, fwd_send, fwd_recv,
    half_send, half_recv, vec_send, vec_recv,
):
    me = lax.axis_index("cells")
    rank = lax.axis_index("rhs")
    near = rank + 1 - 2 * (rank % 2)
    far = (rank + 2) % 4
    far_near = (near + 2) % 4
    blocks, columns, width = own_v.shape
    node = couple_g.shape[0]
    reach = [max(1, 2 ** (level - 2)) for level in range(1, levels + 1)]
    partners = sorted({s % n for d in reach + [1, 2, n // 2] for s in (d, -d)})
    odd = me % 2
    side = 2 * odd - 1
    beside = me - side
    ahead, behind = me + 2 * side, me - 2 * side
    has_ahead = jnp.logical_and(ahead >= 0, ahead < n)
    has_behind = jnp.logical_and(behind >= 0, behind < n)
    ahead, behind = (ahead + n) % n, (behind + n) % n

    DIAG, BESIDE, AHEAD, BEHIND = range(4)
    row_of = (HOP + side, HOP - side, HOP + 2 * side, HOP - 2 * side)

    cells, slots = leaf_couple.shape[0], leaf_couple.shape[1]

    def leaf_copies(c):
        return [
            pltpu.make_async_copy(rhs.at[c], rhs_v.at[c], leaf_sem.at[0, c]),
            pltpu.make_async_copy(inverse.at[c], inverse_v.at[c], leaf_sem.at[1, c]),
            pltpu.make_async_copy(leaf_couple.at[c], leaf_couple_v.at[c], leaf_sem.at[2, c]),
        ]

    for c in range(cells):
        for copy in leaf_copies(c):
            copy.start()

    barrier = pltpu.get_barrier_semaphore()
    for step in partners:
        pl.semaphore_signal(barrier, inc=1, device_id=((me + step) % n, rank), device_id_type=MESH)
    for other in (near, far):
        pl.semaphore_signal(barrier, inc=1, device_id=(me, other), device_id_type=MESH)
    pl.semaphore_wait(barrier, len(partners) + 2)

    def shard(which):
        return pl.ds(pl.multiple_of(which * width, width), width)

    def remote(src, dst, s_sem, r_sem, cell, at):
        return pltpu.make_async_remote_copy(
            src_ref=src, dst_ref=dst, send_sem=s_sem, recv_sem=r_sem,
            device_id=(cell, at), device_id_type=MESH,
        )

    group = blocks // CHUNKS
    depth = lift.shape[0] // CHUNKS
    pieces = [(lift, lift_g, pl.ds(q * depth, depth)) for q in range(CHUNKS)]
    pieces += [(mix, mix_g, pl.ds(0, mix.shape[0])), (couple, couple_g, pl.ds(0, node))]
    count = len(pieces)
    halves = [(mix, mix_h, pl.ds(0, node)), (mix, mix_h, pl.ds(node, node)), (couple, couple_h, pl.ds(0, node))]

    def place(i, which):
        _, dst, rows = (pieces + halves)[i]
        return dst.at[rows, shard(which)]

    def source(i):
        return pieces[i][0].at[pieces[i][2]] if i < count else place(i, rank)

    def to_near(i):
        return remote(source(i), place(i, rank), near_send.at[i], near_recv.at[i], me, near)

    def to_far(i):
        return remote(source(i), place(i, rank), far_send.at[i], far_recv.at[i], me, far)

    def forward(i):
        return remote(place(i, far), place(i, far), fwd_send.at[i], fwd_recv.at[i], me, near)

    def near_arrival(i):
        return remote(place(i, near), place(i, near), near_send.at[i], near_recv.at[i], me, near)

    def far_arrival(i):
        return remote(place(i, far), place(i, far), far_send.at[i], far_recv.at[i], me, far)

    def fwd_arrival(i):
        return remote(place(i, far_near), place(i, far_near), fwd_send.at[i], fwd_recv.at[i], me, near)

    def across(i):
        src, dst, rows = halves[i]
        return remote(
            src.at[rows], dst.at[rows, shard(rank)], half_send.at[i], half_recv.at[i],
            (me + n // 2) % n, rank,
        )

    first_half = CHUNKS // 2

    def rows_of(q):
        return pl.ds(q * group, group)

    def rows_in_half(q):
        return pl.ds((q % first_half) * group, group)

    def diag(q):
        at = 0 if q < first_half else 1
        return remote(
            send.at[DIAG, rows_of(q)], relay.at[at, rows_in_half(q)],
            port_send.at[0, q], port_recv.at[0, q], beside if at == 0 else ahead, rank,
        )

    def to_beside(q):
        return remote(send.at[BESIDE, rows_of(q)], recv.at[0, rows_of(q)], port_send.at[1, q], port_recv.at[1, q], beside, rank)

    def to_ahead(q):
        return remote(
            send.at[AHEAD, rows_of(q)], recv.at[1, rows_of(q)],
            port_send.at[2, q], port_recv.at[2, q], ahead, rank,
        )

    def to_behind(q):
        return remote(send.at[BEHIND, rows_of(q)], recv.at[2, rows_of(q)], port_send.at[3, q], port_recv.at[3, q], behind, rank)

    for i in range(2):
        across(i).start()
    for i in range(count):
        to_far(i).start()
    for i in range(count):
        to_near(i).start()
    locals_ = [pltpu.make_async_copy(skel, skel_v, local_sem.at[0])]
    for i, (src, dst, rows) in enumerate(pieces):
        locals_.append(pltpu.make_async_copy(src.at[rows], dst.at[rows, shard(rank)], local_sem.at[1 + i]))
    for copy in locals_:
        copy.start()

    @pl.loop(0, partial.shape[0])
    def _(i):
        partial[i] = jnp.zeros((columns, width), F32)

    @pl.loop(0, cells)
    def _(c):
        for copy in leaf_copies(c):
            copy.wait()
        solved = dot(rhs_v[c], inverse_v[c]).astype(BF16)
        leaf_v[c] = solved
        for k in range(0, slots, 2):
            pair = [j for j in (k, k + 1) if j < slots]
            update = dot(solved, jnp.concatenate([leaf_couple_v[c, j] for j in pair], axis=1))
            for at, j in enumerate(pair):
                i = c * slots + j
                partial[i] = update[:, at * width : (at + 1) * width] + partial[prev[i]]

    def emit(role, q):
        @pl.loop(q * group, (q + 1) * group)
        def _(b):
            send[role, b] = partial[last_of[row_of[role] * blocks + b]].astype(BF16)

    for at in range(first_half):
        for q in (at, at + first_half):
            emit(DIAG, q)

            @pl.when(has_ahead)
            def _():
                diag(q).start()

        emit(BEHIND, at + first_half)

        @pl.when(has_behind)
        def _():
            to_behind(at + first_half).start()

    for q in range(CHUNKS):
        if q < first_half:
            emit(BESIDE, q)
            to_beside(q).start()
        emit(AHEAD, q)

        @pl.when(has_ahead)
        def _():
            to_ahead(q).start()

    leaf_out = pltpu.make_async_copy(leaf_v, out_leaf, leaf_sem.at[0, 0])
    leaf_out.start()
    for q in range(first_half):
        emit(BEHIND, q)
        emit(BESIDE, q + first_half)

    for slot, there in ((1, has_behind), (2, has_ahead)):
        @pl.when(jnp.logical_not(there))
        def _():
            @pl.loop(0, blocks)
            def _(b):
                recv[slot, b] = jnp.zeros((columns, width), BF16)

    for copy in locals_:
        copy.wait()
    for b in range(blocks):
        own_v[b] = skel_v[pl.ds(b, columns, stride=blocks), :] - partial[last_of[HOP * blocks + b]]

    for at in range(2):
        role = (BEHIND, BESIDE)[at]
        for q in range(at * first_half, (at + 1) * first_half):
            @pl.when(has_behind)
            def _():
                diag(q).wait_recv()

                @pl.loop(q * group, (q + 1) * group)
                def _(b):
                    passing = relay[at, b - at * (blocks // 2)].astype(F32)
                    send[role, b] = (send[role, b].astype(F32) + passing).astype(BF16)

                if at == 0:
                    to_behind(q).start()

            if at == 1:
                to_beside(q).start()
        far_arrival(at).wait_recv()
        forward(at).start()

    def pass_on(i):
        across(i).wait_recv()
        to_far(count + i).start()
        to_near(count + i).start()

    total = None
    for q in range(CHUNKS):
        for i in ([], [2], [3], list(range(CHUNKS, count)))[q]:
            far_arrival(i).wait_recv()
            forward(i).start()
        if q == 1:
            for i in range(2):
                pass_on(i)
        to_beside(q).wait_recv()

        @pl.when(has_behind)
        def _():
            to_ahead(q).wait_recv()

        @pl.when(has_ahead)
        def _():
            to_behind(q).wait_recv()

        if q == CHUNKS - 1:
            across(2).start()
        for b in range(q * group, (q + 1) * group):
            arrived = recv[0, b].astype(F32) + recv[1, b].astype(F32) + recv[2, b].astype(F32)
            value = own_v[b] - arrived
            skel_v[pl.ds(b, columns, stride=blocks), :] = value
            flat[:, b * width : (b + 1) * width] = value.astype(BF16)
        near_arrival(q).wait_recv()
        fwd_arrival(q).wait_recv()
        part = dot(flat[:, q * depth : (q + 1) * depth], lift_g[q * depth : (q + 1) * depth, :])
        total = part if total is None else total + part
    mine[0] = total.astype(BF16)

    def vector(src, dst, at, step):
        return remote(src, dst, vec_send.at[at], vec_recv.at[at], (me + step + n) % n, rank)

    result = pltpu.make_async_copy(skel_v, out_skel, local_sem.at[0])
    sent = []

    def merge(first, second, mixing, coupling):
        solved = (dot(first, mixing[:node, :]) + dot(second, mixing[node:, :])).astype(BF16)
        skeleton = 0.5 * (first.astype(F32) + second.astype(F32)) - dot(solved, coupling[...])
        return solved, skeleton

    for level in range(levels - 1):
        d = reach[level]
        up = vector(mine.at[level], left_v.at[level], 2 * level, d)
        up.start()
        sent.append(up)
        if level > 0:
            down = vector(mine.at[level], right_v.at[level], 2 * level + 1, -d)
            down.start()
            sent.append(down)
        else:
            result.start()
            for i in range(CHUNKS, count):
                near_arrival(i).wait_recv()
                fwd_arrival(i).wait_recv()
            for i in range(count, count + 2):
                far_arrival(i).wait_recv()
                forward(i).start()
        up.wait_recv()
        if level > 0:
            down.wait_recv()
            second = right_v[level]
        else:
            second = mine[0]
        _, skeleton = merge(left_v[level], second, mix_g, couple_g)
        mine[level + 1] = skeleton.astype(BF16)

    last = levels - 1
    up = vector(mine.at[last], left_v.at[last], 2 * last, reach[last])
    down = vector(mine.at[last], right_v.at[last], 2 * last + 1, -reach[last])
    up.start()
    down.start()
    sent += [up, down]
    pass_on(2)
    far_arrival(count + 2).wait_recv()
    forward(count + 2).start()
    up.wait_recv()
    down.wait_recv()
    for i in range(count, count + len(halves)):
        near_arrival(i).wait_recv()
        fwd_arrival(i).wait_recv()
    solved, skeleton = merge(right_v[last], left_v[last], mix_h, couple_h)
    solved, skeleton = merge(skeleton.astype(BF16), solved, mix_g, couple_g)
    out_sol[...] = solved
    out_node[...] = skeleton

    for copy in sent:
        copy.wait_send()
    for i in range(count + len(halves)):
        to_near(i).wait_send()
        to_far(i).wait_send()
        forward(i).wait_send()
    for i in range(len(halves)):
        across(i).wait_send()
    for q in range(CHUNKS):
        to_beside(q).wait_send()

        @pl.when(has_ahead)
        def _():
            diag(q).wait_send()
            to_ahead(q).wait_send()

        @pl.when(has_behind)
        def _():
            to_behind(q).wait_send()

    result.wait()
    leaf_out.wait()


def tree_call(n, blocks, prev, last_of, rhs, inverse, leaf_couple, skel, lift, mix, couple):
    cells, columns, _ = rhs.shape
    slots, width = leaf_couple.shape[1], leaf_couple.shape[3]
    node = couple.shape[0]
    levels = n.bit_length() - 1
    pieces = CHUNKS + 2 + 3
    dma = pltpu.SemaphoreType.DMA
    vmem = pl.BlockSpec(memory_space=pltpu.VMEM)
    hbm = pl.BlockSpec(memory_space=pl.ANY)
    return pl.pallas_call(
        functools.partial(tree_kernel, n, levels),
        out_shape=[
            jax.ShapeDtypeStruct(rhs.shape, BF16),
            jax.ShapeDtypeStruct(skel.shape, F32),
            jax.ShapeDtypeStruct((columns, node), BF16),
            jax.ShapeDtypeStruct((columns, node), F32),
        ],
        in_specs=[pl.BlockSpec(memory_space=pltpu.SMEM)] * 2 + [hbm] * 7,
        out_specs=[hbm, hbm, vmem, vmem],
        scratch_shapes=[
            pltpu.VMEM(rhs.shape, BF16),
            pltpu.VMEM(inverse.shape, BF16),
            pltpu.VMEM(leaf_couple.shape, BF16),
            pltpu.VMEM(rhs.shape, BF16),
            pltpu.VMEM((cells * slots + 1, columns, width), F32),
            pltpu.VMEM((4, blocks, columns, width), BF16),
            pltpu.VMEM((3, blocks, columns, width), BF16),
            pltpu.VMEM((2, blocks // 2, columns, width), BF16),
            pltpu.VMEM((blocks, columns, width), F32),
            pltpu.VMEM(skel.shape, F32),
            pltpu.VMEM((columns, blocks * width), BF16),
            pltpu.VMEM((lift.shape[0], node), BF16),
            pltpu.VMEM((mix.shape[0], node), BF16),
            pltpu.VMEM((couple.shape[0], node), BF16),
            pltpu.VMEM((mix.shape[0], node), BF16),
            pltpu.VMEM((couple.shape[0], node), BF16),
            pltpu.VMEM((levels, columns, node), BF16),
            pltpu.VMEM((levels, columns, node), BF16),
            pltpu.VMEM((levels, columns, node), BF16),
            dma((3, cells)),
            dma((1 + CHUNKS + 2,)),
            dma((4, CHUNKS)),
            dma((4, CHUNKS)),
            dma((pieces,)), dma((pieces,)), dma((pieces,)),
            dma((pieces,)), dma((pieces,)), dma((pieces,)),
            dma((3,)), dma((3,)),
            dma((2 * levels,)),
            dma((2 * levels,)),
        ],
        compiler_params=pltpu.CompilerParams(
            collective_id=0, has_side_effects=True, vmem_limit_bytes=60 * 2**20
        ),
    )(prev, last_of, rhs, inverse, leaf_couple, skel, lift, mix, couple)


def on_device(
    right_side, leaf_inverse, leaf_couple, skel_target, skeleton_in, lift_ops, node_mix, node_couple
):
    position = lax.axis_index("cells")
    n = lax.axis_size("cells")
    columns, blocks, width = skeleton_in.shape
    targets = skel_target.reshape(-1) - (position - HOP) * blocks
    total = targets.shape[0]
    at = jnp.arange(total, dtype=jnp.int32)
    rows = (2 * HOP + 1) * blocks

    def latest(hit):
        found = jnp.max(jnp.where(hit, at[None, :], -1), axis=1)
        return jnp.where(found < 0, total, found)

    prev = latest((targets[None, :] == targets[:, None]) & (at[None, :] < at[:, None]))
    last_of = latest(targets[None, :] == jnp.arange(rows, dtype=jnp.int32)[:, None])
    solved, skel, node_solution, node_skeleton = tree_call(
        n, blocks, prev, last_of, right_side, leaf_inverse, leaf_couple,
        skeleton_in.reshape(columns * blocks, width), lift_ops[0], node_mix[0], node_couple[0],
    )
    return (
        solved,
        skel.reshape(columns, blocks, width),
        node_solution[None],
        node_skeleton[None],
    )


def solution(mesh):
    return jax.shard_map(
        on_device,
        mesh=mesh,
        in_specs=(
            P("cells", "rhs", None),
            P("cells", None, None),
            P("cells", None, None, None),
            P("cells", None),
            P("rhs", "cells", None),
            P("cells", None, "rhs"),
            P("cells", None, "rhs"),
            P("cells", None, "rhs"),
        ),
        out_specs=(
            P("cells", "rhs", None),
            P("rhs", "cells", None),
            P("cells", "rhs", None),
            P("cells", "rhs", None),
        ),
        check_vma=False,
    )
```

```python
import functools

import jax
import jax.numpy as jnp
from jax import lax
from jax.experimental import pallas as pl
from jax.experimental.pallas import tpu as pltpu
from jax.sharding import PartitionSpec as P

HOP = 2
CHUNKS = 4
MESH = pl.DeviceIdType.MESH
F32, BF16 = jnp.float32, jnp.bfloat16


def dot(a, b):
    return jnp.dot(a, b, preferred_element_type=F32)


def tree_kernel(
    n, levels, target, rhs, inverse, leaf_couple, skel, lift, mix, couple,
    out_leaf, out_skel, out_sol, out_node,
    table_v, table, rhs_v, inverse_v, leaf_couple_v, leaf_v, partial, send, recv, relay, own_v, skel_v, flat, lift_g, mix_g, couple_g, mix_h, couple_h,
    mine, left_v, right_v,
    table_sem, leaf_sem, local_sem, port_send, port_recv, near_send, near_recv, far_send, far_recv, fwd_send, fwd_recv,
    half_send, half_recv, vec_send, vec_recv,
):
    me = lax.axis_index("cells")
    rank = lax.axis_index("rhs")
    near = rank + 1 - 2 * (rank % 2)
    far = (rank + 2) % 4
    far_near = (near + 2) % 4
    blocks, columns, width = own_v.shape
    node = couple_g.shape[0]
    reach = [max(1, 2 ** (level - 2)) for level in range(1, levels + 1)]
    partners = sorted({s % n for d in reach + [1, 2, n // 2] for s in (d, -d)})
    odd = me % 2
    side = 2 * odd - 1
    beside = me - side
    ahead, behind = me + 2 * side, me - 2 * side
    has_ahead = jnp.logical_and(ahead >= 0, ahead < n)
    has_behind = jnp.logical_and(behind >= 0, behind < n)
    ahead, behind = (ahead + n) % n, (behind + n) % n

    DIAG, BESIDE, AHEAD, BEHIND = range(4)
    row_of = (HOP + side, HOP - side, HOP + 2 * side, HOP - 2 * side)

    cells, slots = leaf_couple.shape[0], leaf_couple.shape[1]

    def leaf_copies(c):
        return [
            pltpu.make_async_copy(rhs.at[c], rhs_v.at[c], leaf_sem.at[0, c]),
            pltpu.make_async_copy(inverse.at[c], inverse_v.at[c], leaf_sem.at[1, c]),
            pltpu.make_async_copy(leaf_couple.at[c], leaf_couple_v.at[c], leaf_sem.at[2, c]),
        ]

    for c in range(cells):
        for copy in leaf_copies(c):
            copy.start()

    total = cells * slots
    lanes = table_v.shape[1]
    lane = lax.broadcasted_iota(jnp.int32, (1, lanes), 1)
    block = lane + (me - HOP) * blocks
    names = [target[i // slots, i % slots] for i in range(total)]
    named = jnp.full((1, lanes), -1, jnp.int32)
    for i in range(total):
        named = jnp.where(lane == i, names[i], named)
    before = last = jnp.full((1, lanes), total, jnp.int32)
    for i in range(total):
        before = jnp.where(jnp.logical_and(named == names[i], lane > i), i, before)
        last = jnp.where(block == names[i], i, last)
    table_v[...] = jnp.zeros(table_v.shape, jnp.int32)
    table_v[0:1, :] = before
    table_v[1:2, :] = last
    table_copy = pltpu.make_async_copy(table_v, table, table_sem)
    table_copy.start()

    barrier = pltpu.get_barrier_semaphore()
    for step in partners:
        pl.semaphore_signal(barrier, inc=1, device_id=((me + step) % n, rank), device_id_type=MESH)
    for other in (near, far):
        pl.semaphore_signal(barrier, inc=1, device_id=(me, other), device_id_type=MESH)
    pl.semaphore_wait(barrier, len(partners) + 2)

    def shard(which):
        return pl.ds(pl.multiple_of(which * width, width), width)

    def remote(src, dst, s_sem, r_sem, cell, at):
        return pltpu.make_async_remote_copy(
            src_ref=src, dst_ref=dst, send_sem=s_sem, recv_sem=r_sem,
            device_id=(cell, at), device_id_type=MESH,
        )

    group = blocks // CHUNKS
    depth = lift.shape[0] // CHUNKS
    pieces = [(lift, lift_g, pl.ds(q * depth, depth)) for q in range(CHUNKS)]
    pieces += [(mix, mix_g, pl.ds(0, mix.shape[0])), (couple, couple_g, pl.ds(0, node))]
    count = len(pieces)
    halves = [(mix, mix_h, pl.ds(0, node)), (mix, mix_h, pl.ds(node, node)), (couple, couple_h, pl.ds(0, node))]

    def place(i, which):
        _, dst, rows = (pieces + halves)[i]
        return dst.at[rows, shard(which)]

    def source(i):
        return pieces[i][0].at[pieces[i][2]] if i < count else place(i, rank)

    def to_near(i):
        return remote(source(i), place(i, rank), near_send.at[i], near_recv.at[i], me, near)

    def to_far(i):
        return remote(source(i), place(i, rank), far_send.at[i], far_recv.at[i], me, far)

    def forward(i):
        return remote(place(i, far), place(i, far), fwd_send.at[i], fwd_recv.at[i], me, near)

    def near_arrival(i):
        return remote(place(i, near), place(i, near), near_send.at[i], near_recv.at[i], me, near)

    def far_arrival(i):
        return remote(place(i, far), place(i, far), far_send.at[i], far_recv.at[i], me, far)

    def fwd_arrival(i):
        return remote(place(i, far_near), place(i, far_near), fwd_send.at[i], fwd_recv.at[i], me, near)

    def across(i):
        src, dst, rows = halves[i]
        return remote(
            src.at[rows], dst.at[rows, shard(rank)], half_send.at[i], half_recv.at[i],
            (me + n // 2) % n, rank,
        )

    first_half = CHUNKS // 2

    def rows_of(q):
        return pl.ds(q * group, group)

    def rows_in_half(q):
        return pl.ds((q % first_half) * group, group)

    def diag(q):
        at = 0 if q < first_half else 1
        return remote(
            send.at[DIAG, rows_of(q)], relay.at[at, rows_in_half(q)],
            port_send.at[0, q], port_recv.at[0, q], beside if at == 0 else ahead, rank,
        )

    def to_beside(q):
        return remote(send.at[BESIDE, rows_of(q)], recv.at[0, rows_of(q)], port_send.at[1, q], port_recv.at[1, q], beside, rank)

    def to_ahead(q):
        return remote(
            send.at[AHEAD, rows_of(q)], recv.at[1, rows_of(q)],
            port_send.at[2, q], port_recv.at[2, q], ahead, rank,
        )

    def to_behind(q):
        return remote(send.at[BEHIND, rows_of(q)], recv.at[2, rows_of(q)], port_send.at[3, q], port_recv.at[3, q], behind, rank)

    for i in range(2):
        across(i).start()
    for i in range(count):
        to_far(i).start()
    for i in range(count):
        to_near(i).start()
    locals_ = [pltpu.make_async_copy(skel, skel_v, local_sem.at[0])]
    for i, (src, dst, rows) in enumerate(pieces):
        locals_.append(pltpu.make_async_copy(src.at[rows], dst.at[rows, shard(rank)], local_sem.at[1 + i]))
    for copy in locals_:
        copy.start()

    @pl.loop(0, partial.shape[0])
    def _(i):
        partial[i] = jnp.zeros((columns, width), F32)

    table_copy.wait()

    @pl.loop(0, cells)
    def _(c):
        for copy in leaf_copies(c):
            copy.wait()
        solved = dot(rhs_v[c], inverse_v[c]).astype(BF16)
        leaf_v[c] = solved
        for k in range(0, slots, 2):
            pair = [j for j in (k, k + 1) if j < slots]
            update = dot(solved, jnp.concatenate([leaf_couple_v[c, j] for j in pair], axis=1))
            for at, j in enumerate(pair):
                i = c * slots + j
                partial[i] = update[:, at * width : (at + 1) * width] + partial[table[0, i]]

    def emit(role, q):
        @pl.loop(q * group, (q + 1) * group)
        def _(b):
            send[role, b] = partial[table[1, row_of[role] * blocks + b]].astype(BF16)

    for at in range(first_half):
        for q in (at, at + first_half):
            emit(DIAG, q)

            @pl.when(has_ahead)
            def _():
                diag(q).start()

        emit(BEHIND, at + first_half)

        @pl.when(has_behind)
        def _():
            to_behind(at + first_half).start()

    for q in range(CHUNKS):
        if q < first_half:
            emit(BESIDE, q)
            to_beside(q).start()
        emit(AHEAD, q)

        @pl.when(has_ahead)
        def _():
            to_ahead(q).start()

    leaf_out = pltpu.make_async_copy(leaf_v, out_leaf, leaf_sem.at[0, 0])
    leaf_out.start()
    for q in range(first_half):
        emit(BEHIND, q)
        emit(BESIDE, q + first_half)

    for slot, there in ((1, has_behind), (2, has_ahead)):
        @pl.when(jnp.logical_not(there))
        def _():
            @pl.loop(0, blocks)
            def _(b):
                recv[slot, b] = jnp.zeros((columns, width), BF16)

    for copy in locals_:
        copy.wait()
    for b in range(blocks):
        own_v[b] = skel_v[pl.ds(b, columns, stride=blocks), :] - partial[table[1, HOP * blocks + b]]

    for at in range(2):
        role = (BEHIND, BESIDE)[at]
        for q in range(at * first_half, (at + 1) * first_half):
            @pl.when(has_behind)
            def _():
                diag(q).wait_recv()

                @pl.loop(q * group, (q + 1) * group)
                def _(b):
                    passing = relay[at, b - at * (blocks // 2)].astype(F32)
                    send[role, b] = (send[role, b].astype(F32) + passing).astype(BF16)

                if at == 0:
                    to_behind(q).start()

            if at == 1:
                to_beside(q).start()
        far_arrival(at).wait_recv()
        forward(at).start()

    def pass_on(i):
        across(i).wait_recv()
        to_far(count + i).start()
        to_near(count + i).start()

    total = None
    for q in range(CHUNKS):
        for i in ([], [2], [3], list(range(CHUNKS, count)))[q]:
            far_arrival(i).wait_recv()
            forward(i).start()
        if q == 1:
            for i in range(2):
                pass_on(i)
        to_beside(q).wait_recv()

        @pl.when(has_behind)
        def _():
            to_ahead(q).wait_recv()

        @pl.when(has_ahead)
        def _():
            to_behind(q).wait_recv()

        if q == CHUNKS - 1:
            across(2).start()
        for b in range(q * group, (q + 1) * group):
            arrived = recv[0, b].astype(F32) + recv[1, b].astype(F32) + recv[2, b].astype(F32)
            value = own_v[b] - arrived
            if q < CHUNKS - 1:
                skel_v[pl.ds(b, columns, stride=blocks), :] = value
            else:
                own_v[b] = value
            flat[:, b * width : (b + 1) * width] = value.astype(BF16)
        near_arrival(q).wait_recv()
        fwd_arrival(q).wait_recv()
        part = dot(flat[:, q * depth : (q + 1) * depth], lift_g[q * depth : (q + 1) * depth, :])
        total = part if total is None else total + part
    mine[0] = total.astype(BF16)

    def vector(src, dst, at, step):
        return remote(src, dst, vec_send.at[at], vec_recv.at[at], (me + step + n) % n, rank)

    result = pltpu.make_async_copy(skel_v, out_skel, local_sem.at[0])
    sent = []

    def merge(first, second, mixing, coupling, mixed=None):
        if mixed is None:
            mixed = dot(second, mixing[node:, :])
        solved = (dot(first, mixing[:node, :]) + mixed).astype(BF16)
        skeleton = 0.5 * (first.astype(F32) + second.astype(F32)) - dot(solved, coupling[...])
        return solved, skeleton

    for level in range(levels - 1):
        d = reach[level]
        up = vector(mine.at[level], left_v.at[level], 2 * level, d)
        up.start()
        sent.append(up)
        if level > 0:
            down = vector(mine.at[level], right_v.at[level], 2 * level + 1, -d)
            down.start()
            sent.append(down)
        else:
            for b in range((CHUNKS - 1) * group, blocks):
                skel_v[pl.ds(b, columns, stride=blocks), :] = own_v[b]
            result.start()
            for i in range(CHUNKS, count):
                near_arrival(i).wait_recv()
                fwd_arrival(i).wait_recv()
            second = mine[0]
            mixed = dot(second, mix_g[node:, :])
            for i in range(count, count + 2):
                far_arrival(i).wait_recv()
                forward(i).start()
        if level > 0:
            down.wait_recv()
            second = right_v[level]
            mixed = dot(second, mix_g[node:, :])
        up.wait_recv()
        _, skeleton = merge(left_v[level], second, mix_g, couple_g, mixed)
        mine[level + 1] = skeleton.astype(BF16)

    last = levels - 1
    up = vector(mine.at[last], left_v.at[last], 2 * last, reach[last])
    down = vector(mine.at[last], right_v.at[last], 2 * last + 1, -reach[last])
    up.start()
    down.start()
    sent += [up, down]
    pass_on(2)
    far_arrival(count + 2).wait_recv()
    forward(count + 2).start()
    up.wait_recv()
    down.wait_recv()
    for i in range(count, count + len(halves)):
        near_arrival(i).wait_recv()
        fwd_arrival(i).wait_recv()
    solved, skeleton = merge(right_v[last], left_v[last], mix_h, couple_h)
    solved, skeleton = merge(skeleton.astype(BF16), solved, mix_g, couple_g)
    out_sol[...] = solved
    out_node[...] = skeleton

    for copy in sent:
        copy.wait_send()
    for i in range(count + len(halves)):
        to_near(i).wait_send()
        to_far(i).wait_send()
        forward(i).wait_send()
    for i in range(len(halves)):
        across(i).wait_send()
    for q in range(CHUNKS):
        to_beside(q).wait_send()

        @pl.when(has_ahead)
        def _():
            diag(q).wait_send()
            to_ahead(q).wait_send()

        @pl.when(has_behind)
        def _():
            to_behind(q).wait_send()

    result.wait()
    leaf_out.wait()


def tree_call(n, blocks, target, rhs, inverse, leaf_couple, skel, lift, mix, couple):
    cells, columns, _ = rhs.shape
    slots, width = leaf_couple.shape[1], leaf_couple.shape[3]
    node = couple.shape[0]
    levels = n.bit_length() - 1
    pieces = CHUNKS + 2 + 3
    lanes = -(-max(cells * slots, (2 * HOP + 1) * blocks) // 128) * 128
    dma = pltpu.SemaphoreType.DMA
    vmem = pl.BlockSpec(memory_space=pltpu.VMEM)
    hbm = pl.BlockSpec(memory_space=pl.ANY)
    return pl.pallas_call(
        functools.partial(tree_kernel, n, levels),
        out_shape=[
            jax.ShapeDtypeStruct(rhs.shape, BF16),
            jax.ShapeDtypeStruct(skel.shape, F32),
            jax.ShapeDtypeStruct((columns, node), BF16),
            jax.ShapeDtypeStruct((columns, node), F32),
        ],
        in_specs=[pl.BlockSpec(memory_space=pltpu.SMEM)] + [hbm] * 7,
        out_specs=[hbm, hbm, vmem, vmem],
        scratch_shapes=[
            pltpu.VMEM((8, lanes), jnp.int32),
            pltpu.SMEM((8, lanes), jnp.int32),
            pltpu.VMEM(rhs.shape, BF16),
            pltpu.VMEM(inverse.shape, BF16),
            pltpu.VMEM(leaf_couple.shape, BF16),
            pltpu.VMEM(rhs.shape, BF16),
            pltpu.VMEM((cells * slots + 1, columns, width), F32),
            pltpu.VMEM((4, blocks, columns, width), BF16),
            pltpu.VMEM((3, blocks, columns, width), BF16),
            pltpu.VMEM((2, blocks // 2, columns, width), BF16),
            pltpu.VMEM((blocks, columns, width), F32),
            pltpu.VMEM(skel.shape, F32),
            pltpu.VMEM((columns, blocks * width), BF16),
            pltpu.VMEM((lift.shape[0], node), BF16),
            pltpu.VMEM((mix.shape[0], node), BF16),
            pltpu.VMEM((couple.shape[0], node), BF16),
            pltpu.VMEM((mix.shape[0], node), BF16),
            pltpu.VMEM((couple.shape[0], node), BF16),
            pltpu.VMEM((levels, columns, node), BF16),
            pltpu.VMEM((levels, columns, node), BF16),
            pltpu.VMEM((levels, columns, node), BF16),
            dma,
            dma((3, cells)),
            dma((1 + CHUNKS + 2,)),
            dma((4, CHUNKS)),
            dma((4, CHUNKS)),
            dma((pieces,)), dma((pieces,)), dma((pieces,)),
            dma((pieces,)), dma((pieces,)), dma((pieces,)),
            dma((3,)), dma((3,)),
            dma((2 * levels,)),
            dma((2 * levels,)),
        ],
        compiler_params=pltpu.CompilerParams(
            collective_id=0, has_side_effects=True, vmem_limit_bytes=60 * 2**20
        ),
    )(target, rhs, inverse, leaf_couple, skel, lift, mix, couple)


def hand_out_kernel(cuts, *refs):
    count = len(cuts)
    sems = refs[-1]
    copies = []
    for src, dst, cut in zip(refs[:count], refs[count : 2 * count], cuts):
        rows = src.shape[0] // cut
        for i in range(cut):
            part = pl.ds(i * rows, rows)
            copies.append(pltpu.make_async_copy(src.at[part], dst.at[part], sems.at[len(copies)]))
    for copy in copies:
        copy.start()
    for copy in copies:
        copy.wait()


def hand_out(*arrays):
    cuts = (4, 8, 1, 2)
    hbm = pl.BlockSpec(memory_space=pl.ANY)
    return pl.pallas_call(
        functools.partial(hand_out_kernel, cuts),
        out_shape=[jax.ShapeDtypeStruct(a.shape, a.dtype) for a in arrays],
        in_specs=[hbm] * len(arrays),
        out_specs=[hbm] * len(arrays),
        scratch_shapes=[pltpu.SemaphoreType.DMA((sum(cuts),))],
        compiler_params=pltpu.CompilerParams(vmem_limit_bytes=60 * 2**20),
    )(*arrays)


def on_device(
    right_side, leaf_inverse, leaf_couple, skel_target, skeleton_in, lift_ops, node_mix, node_couple
):
    n = lax.axis_size("cells")
    columns, blocks, width = skeleton_in.shape
    solved, skel, node_solution, node_skeleton = hand_out(
        *tree_call(
            n, blocks, skel_target, right_side, leaf_inverse, leaf_couple,
            skeleton_in.reshape(columns * blocks, width), lift_ops[0], node_mix[0], node_couple[0],
        )
    )
    return (
        solved,
        skel.reshape(columns, blocks, width),
        node_solution[None],
        node_skeleton[None],
    )


def solution(mesh):
    return jax.shard_map(
        on_device,
        mesh=mesh,
        in_specs=(
            P("cells", "rhs", None),
            P("cells", None, None),
            P("cells", None, None, None),
            P("cells", None),
            P("rhs", "cells", None),
            P("cells", None, "rhs"),
            P("cells", None, "rhs"),
            P("cells", None, "rhs"),
        ),
        out_specs=(
            P("cells", "rhs", None),
            P("rhs", "cells", None),
            P("cells", "rhs", None),
            P("cells", "rhs", None),
        ),
        check_vma=False,
    )
```

```python
import functools

import jax
import jax.numpy as jnp
from jax import lax
from jax.experimental import pallas as pl
from jax.experimental.pallas import tpu as pltpu
from jax.sharding import PartitionSpec as P

HOP = 2
CHUNKS = 4
PIECES = 4
MESH = pl.DeviceIdType.MESH
F32, BF16 = jnp.float32, jnp.bfloat16


def dot(a, b):
    return jnp.dot(a, b, preferred_element_type=F32)


def tree_kernel(
    n, levels, target, rhs, inverse, leaf_couple, skel, lift, mix, couple,
    out_leaf, out_skel, out_sol, out_node,
    table_v, table, rhs_v, inverse_v, leaf_couple_v, leaf_v, partial, send, recv, relay, own_v, skel_v, flat, lift_g, mix_g, couple_g, mix_h, couple_h,
    mine, left_v, right_v, pair_v,
    table_sem, leaf_sem, local_sem, port_send, port_recv, near_send, near_recv, far_send, far_recv, fwd_send, fwd_recv,
    half_send, half_recv, vec_send, vec_recv, pair_send, pair_recv,
):
    me = lax.axis_index("cells")
    rank = lax.axis_index("rhs")
    near = rank + 1 - 2 * (rank % 2)
    far = (rank + 2) % 4
    far_near = (near + 2) % 4
    blocks, columns, width = own_v.shape
    node = couple_g.shape[0]
    reach = [max(1, 2 ** (level - 2)) for level in range(1, levels + 1)]
    partners = sorted({s % n for d in reach + [1, 2, n // 2] for s in (d, -d)})
    odd = me % 2
    side = 2 * odd - 1
    beside = me - side
    ahead, behind = me + 2 * side, me - 2 * side
    has_ahead = jnp.logical_and(ahead >= 0, ahead < n)
    has_behind = jnp.logical_and(behind >= 0, behind < n)
    ahead, behind = (ahead + n) % n, (behind + n) % n

    DIAG, BESIDE, AHEAD, BEHIND = range(4)
    row_of = (HOP + side, HOP - side, HOP + 2 * side, HOP - 2 * side)

    cells, slots = leaf_couple.shape[0], leaf_couple.shape[1]

    def leaf_copies(c):
        return [
            pltpu.make_async_copy(rhs.at[c], rhs_v.at[c], leaf_sem.at[0, c]),
            pltpu.make_async_copy(inverse.at[c], inverse_v.at[c], leaf_sem.at[1, c]),
            pltpu.make_async_copy(leaf_couple.at[c], leaf_couple_v.at[c], leaf_sem.at[2, c]),
        ]

    for c in range(cells):
        for copy in leaf_copies(c):
            copy.start()

    total = cells * slots
    lanes = table_v.shape[1]
    lane = lax.broadcasted_iota(jnp.int32, (1, lanes), 1)
    block = lane + (me - HOP) * blocks
    names = [target[i // slots, i % slots] for i in range(total)]
    named = jnp.full((1, lanes), -1, jnp.int32)
    for i in range(total):
        named = jnp.where(lane == i, names[i], named)
    before = last = jnp.full((1, lanes), total, jnp.int32)
    for i in range(total):
        before = jnp.where(jnp.logical_and(named == names[i], lane > i), i, before)
        last = jnp.where(block == names[i], i, last)
    table_v[...] = jnp.zeros(table_v.shape, jnp.int32)
    table_v[0:1, :] = before
    table_v[1:2, :] = last
    table_copy = pltpu.make_async_copy(table_v, table, table_sem)
    table_copy.start()

    barrier = pltpu.get_barrier_semaphore()
    for step in partners:
        pl.semaphore_signal(barrier, inc=1, device_id=((me + step) % n, rank), device_id_type=MESH)
    for other in (near, far):
        pl.semaphore_signal(barrier, inc=1, device_id=(me, other), device_id_type=MESH)
    pl.semaphore_wait(barrier, len(partners) + 2)

    def shard(which):
        return pl.ds(pl.multiple_of(which * width, width), width)

    def remote(src, dst, s_sem, r_sem, cell, at):
        return pltpu.make_async_remote_copy(
            src_ref=src, dst_ref=dst, send_sem=s_sem, recv_sem=r_sem,
            device_id=(cell, at), device_id_type=MESH,
        )

    group = blocks // CHUNKS
    depth = lift.shape[0] // CHUNKS
    pieces = [(lift, lift_g, pl.ds(q * depth, depth)) for q in range(CHUNKS)]
    pieces += [(mix, mix_g, pl.ds(0, mix.shape[0])), (couple, couple_g, pl.ds(0, node))]
    count = len(pieces)
    halves = [(mix, mix_h, pl.ds(0, node)), (mix, mix_h, pl.ds(node, node)), (couple, couple_h, pl.ds(0, node))]

    def place(i, which):
        _, dst, rows = (pieces + halves)[i]
        return dst.at[rows, shard(which)]

    def source(i):
        return pieces[i][0].at[pieces[i][2]] if i < count else place(i, rank)

    def to_near(i):
        return remote(source(i), place(i, rank), near_send.at[i], near_recv.at[i], me, near)

    def to_far(i):
        return remote(source(i), place(i, rank), far_send.at[i], far_recv.at[i], me, far)

    def forward(i):
        return remote(place(i, far), place(i, far), fwd_send.at[i], fwd_recv.at[i], me, near)

    def near_arrival(i):
        return remote(place(i, near), place(i, near), near_send.at[i], near_recv.at[i], me, near)

    def far_arrival(i):
        return remote(place(i, far), place(i, far), far_send.at[i], far_recv.at[i], me, far)

    def fwd_arrival(i):
        return remote(place(i, far_near), place(i, far_near), fwd_send.at[i], fwd_recv.at[i], me, near)

    def across(i):
        src, dst, rows = halves[i]
        return remote(
            src.at[rows], dst.at[rows, shard(rank)], half_send.at[i], half_recv.at[i],
            (me + n // 2) % n, rank,
        )

    first_half = CHUNKS // 2

    def rows_of(q):
        return pl.ds(q * group, group)

    def rows_in_half(q):
        return pl.ds((q % first_half) * group, group)

    def diag(q):
        at = 0 if q < first_half else 1
        return remote(
            send.at[DIAG, rows_of(q)], relay.at[at, rows_in_half(q)],
            port_send.at[0, q], port_recv.at[0, q], beside if at == 0 else ahead, rank,
        )

    def to_beside(q):
        return remote(send.at[BESIDE, rows_of(q)], recv.at[0, rows_of(q)], port_send.at[1, q], port_recv.at[1, q], beside, rank)

    def to_ahead(q):
        return remote(
            send.at[AHEAD, rows_of(q)], recv.at[1, rows_of(q)],
            port_send.at[2, q], port_recv.at[2, q], ahead, rank,
        )

    def to_behind(q):
        return remote(send.at[BEHIND, rows_of(q)], recv.at[2, rows_of(q)], port_send.at[3, q], port_recv.at[3, q], behind, rank)

    for i in range(2):
        across(i).start()
    for i in range(count):
        to_far(i).start()
    for i in range(count):
        to_near(i).start()
    locals_ = [pltpu.make_async_copy(skel, skel_v, local_sem.at[0])]
    for i, (src, dst, rows) in enumerate(pieces):
        locals_.append(pltpu.make_async_copy(src.at[rows], dst.at[rows, shard(rank)], local_sem.at[1 + i]))
    for copy in locals_:
        copy.start()

    @pl.loop(0, partial.shape[0])
    def _(i):
        partial[i] = jnp.zeros((columns, width), F32)

    table_copy.wait()

    @pl.loop(0, cells)
    def _(c):
        for copy in leaf_copies(c):
            copy.wait()
        solved = dot(rhs_v[c], inverse_v[c]).astype(BF16)
        leaf_v[c] = solved
        for k in range(0, slots, 2):
            pair = [j for j in (k, k + 1) if j < slots]
            update = dot(solved, jnp.concatenate([leaf_couple_v[c, j] for j in pair], axis=1))
            for at, j in enumerate(pair):
                i = c * slots + j
                partial[i] = update[:, at * width : (at + 1) * width] + partial[table[0, i]]

    def emit(role, q):
        @pl.loop(q * group, (q + 1) * group)
        def _(b):
            send[role, b] = partial[table[1, row_of[role] * blocks + b]].astype(BF16)

    for at in range(first_half):
        for q in (at, at + first_half):
            emit(DIAG, q)

            @pl.when(has_ahead)
            def _():
                diag(q).start()

        emit(BEHIND, at + first_half)

        @pl.when(has_behind)
        def _():
            to_behind(at + first_half).start()

    for q in range(CHUNKS):
        if q < first_half:
            emit(BESIDE, q)
            to_beside(q).start()
        emit(AHEAD, q)

        @pl.when(has_ahead)
        def _():
            to_ahead(q).start()

    leaf_out = pltpu.make_async_copy(leaf_v, out_leaf, leaf_sem.at[0, 0])
    leaf_out.start()
    for q in range(first_half):
        emit(BEHIND, q)
        emit(BESIDE, q + first_half)

    for slot, there in ((1, has_behind), (2, has_ahead)):
        @pl.when(jnp.logical_not(there))
        def _():
            @pl.loop(0, blocks)
            def _(b):
                recv[slot, b] = jnp.zeros((columns, width), BF16)

    for copy in locals_:
        copy.wait()
    for b in range(blocks):
        own_v[b] = skel_v[pl.ds(b, columns, stride=blocks), :] - partial[table[1, HOP * blocks + b]]

    for at in range(2):
        role = (BEHIND, BESIDE)[at]
        for q in range(at * first_half, (at + 1) * first_half):
            @pl.when(has_behind)
            def _():
                diag(q).wait_recv()

                @pl.loop(q * group, (q + 1) * group)
                def _(b):
                    passing = relay[at, b - at * (blocks // 2)].astype(F32)
                    send[role, b] = (send[role, b].astype(F32) + passing).astype(BF16)

                if at == 0:
                    to_behind(q).start()

            if at == 1:
                to_beside(q).start()
        far_arrival(at).wait_recv()
        forward(at).start()

    def pass_on(i):
        across(i).wait_recv()
        to_far(count + i).start()
        to_near(count + i).start()

    total = None
    for q in range(CHUNKS):
        for i in ([], [2], [3], list(range(CHUNKS, count)))[q]:
            far_arrival(i).wait_recv()
            forward(i).start()
        if q == 1:
            for i in range(2):
                pass_on(i)
        to_beside(q).wait_recv()

        @pl.when(has_behind)
        def _():
            to_ahead(q).wait_recv()

        @pl.when(has_ahead)
        def _():
            to_behind(q).wait_recv()

        if q == CHUNKS - 1:
            across(2).start()
        for b in range(q * group, (q + 1) * group):
            arrived = recv[0, b].astype(F32) + recv[1, b].astype(F32) + recv[2, b].astype(F32)
            value = own_v[b] - arrived
            if q < CHUNKS - 1:
                skel_v[pl.ds(b, columns, stride=blocks), :] = value
            else:
                own_v[b] = value
            flat[:, b * width : (b + 1) * width] = value.astype(BF16)
        near_arrival(q).wait_recv()
        fwd_arrival(q).wait_recv()
        part = dot(flat[:, q * depth : (q + 1) * depth], lift_g[q * depth : (q + 1) * depth, :])
        total = part if total is None else total + part
    mine[0] = total.astype(BF16)

    def vector(src, dst, at, step):
        return remote(src, dst, vec_send.at[at], vec_recv.at[at], (me + step + n) % n, rank)

    result = pltpu.make_async_copy(skel_v, out_skel, local_sem.at[0])
    sent = []

    def merge(first, second, mixing, coupling, mixed=None):
        if mixed is None:
            mixed = dot(second, mixing[node:, :])
        solved = (dot(first, mixing[:node, :]) + mixed).astype(BF16)
        skeleton = 0.5 * (first.astype(F32) + second.astype(F32)) - dot(solved, coupling[...])
        return solved, skeleton

    def next_to(level, skeleton):
        mine[level + 1] = skeleton.astype(BF16)

    up = vector(mine.at[0], left_v.at[0], 0, 1)
    up.start()
    sent.append(up)
    for b in range((CHUNKS - 1) * group, blocks):
        skel_v[pl.ds(b, columns, stride=blocks), :] = own_v[b]
    result.start()
    for i in range(CHUNKS, count):
        near_arrival(i).wait_recv()
        fwd_arrival(i).wait_recv()
    mixed = dot(mine[0], mix_g[node:, :])
    for i in range(count, count + 2):
        far_arrival(i).wait_recv()
        forward(i).start()
    up.wait_recv()
    next_to(0, merge(left_v[0], mine[0], mix_g, couple_g, mixed)[1])

    rows = columns // PIECES
    parts = [pl.ds(i * rows, rows) for i in range(PIECES)]

    def over(i):
        return remote(mine.at[1, parts[i]], pair_v.at[0, parts[i]], pair_send.at[0, i], pair_recv.at[0, i], beside, rank)

    def onward(i):
        return remote(pair_v.at[0, parts[i]], pair_v.at[1, parts[i]], pair_send.at[1, i], pair_recv.at[1, i], behind, rank)

    for i in range(PIECES):
        over(i).start()
    for i in range(PIECES):
        over(i).wait_recv()
        onward(i).start()
    mixed = dot(pair_v[0], mix_g[pl.ds(pl.multiple_of((1 - odd) * node, node), node), :])
    for i in range(PIECES):
        onward(i).wait_recv()
    solved = (mixed + dot(pair_v[1], mix_g[pl.ds(pl.multiple_of(odd * node, node), node), :])).astype(BF16)
    skeleton = 0.5 * (pair_v[0].astype(F32) + pair_v[1].astype(F32)) - dot(solved, couple_g[...])
    next_to(1, skeleton)

    for level in range(2, levels - 1):
        d = reach[level]
        up = vector(mine.at[level], left_v.at[level], 2 * level, d)
        up.start()
        down = vector(mine.at[level], right_v.at[level], 2 * level + 1, -d)
        down.start()
        sent += [up, down]
        down.wait_recv()
        mixed = dot(right_v[level], mix_g[node:, :])
        up.wait_recv()
        next_to(level, merge(left_v[level], right_v[level], mix_g, couple_g, mixed)[1])

    last = levels - 1
    up = vector(mine.at[last], left_v.at[last], 2 * last, reach[last])
    down = vector(mine.at[last], right_v.at[last], 2 * last + 1, -reach[last])
    up.start()
    down.start()
    sent += [up, down]
    pass_on(2)
    far_arrival(count + 2).wait_recv()
    forward(count + 2).start()
    up.wait_recv()
    down.wait_recv()
    for i in range(count, count + len(halves)):
        near_arrival(i).wait_recv()
        fwd_arrival(i).wait_recv()
    solved, skeleton = merge(right_v[last], left_v[last], mix_h, couple_h)
    solved, skeleton = merge(skeleton.astype(BF16), solved, mix_g, couple_g)
    out_sol[...] = solved
    out_node[...] = skeleton

    for copy in sent:
        copy.wait_send()
    for i in range(PIECES):
        over(i).wait_send()
        onward(i).wait_send()
    for i in range(count + len(halves)):
        to_near(i).wait_send()
        to_far(i).wait_send()
        forward(i).wait_send()
    for i in range(len(halves)):
        across(i).wait_send()
    for q in range(CHUNKS):
        to_beside(q).wait_send()

        @pl.when(has_ahead)
        def _():
            diag(q).wait_send()
            to_ahead(q).wait_send()

        @pl.when(has_behind)
        def _():
            to_behind(q).wait_send()

    result.wait()
    leaf_out.wait()


def tree_call(n, blocks, target, rhs, inverse, leaf_couple, skel, lift, mix, couple):
    cells, columns, _ = rhs.shape
    slots, width = leaf_couple.shape[1], leaf_couple.shape[3]
    node = couple.shape[0]
    levels = n.bit_length() - 1
    pieces = CHUNKS + 2 + 3
    lanes = -(-max(cells * slots, (2 * HOP + 1) * blocks) // 128) * 128
    dma = pltpu.SemaphoreType.DMA
    vmem = pl.BlockSpec(memory_space=pltpu.VMEM)
    hbm = pl.BlockSpec(memory_space=pl.ANY)
    return pl.pallas_call(
        functools.partial(tree_kernel, n, levels),
        out_shape=[
            jax.ShapeDtypeStruct(rhs.shape, BF16),
            jax.ShapeDtypeStruct(skel.shape, F32),
            jax.ShapeDtypeStruct((columns, node), BF16),
            jax.ShapeDtypeStruct((columns, node), F32),
        ],
        in_specs=[pl.BlockSpec(memory_space=pltpu.SMEM)] + [hbm] * 7,
        out_specs=[hbm, hbm, vmem, vmem],
        scratch_shapes=[
            pltpu.VMEM((8, lanes), jnp.int32),
            pltpu.SMEM((8, lanes), jnp.int32),
            pltpu.VMEM(rhs.shape, BF16),
            pltpu.VMEM(inverse.shape, BF16),
            pltpu.VMEM(leaf_couple.shape, BF16),
            pltpu.VMEM(rhs.shape, BF16),
            pltpu.VMEM((cells * slots + 1, columns, width), F32),
            pltpu.VMEM((4, blocks, columns, width), BF16),
            pltpu.VMEM((3, blocks, columns, width), BF16),
            pltpu.VMEM((2, blocks // 2, columns, width), BF16),
            pltpu.VMEM((blocks, columns, width), F32),
            pltpu.VMEM(skel.shape, F32),
            pltpu.VMEM((columns, blocks * width), BF16),
            pltpu.VMEM((lift.shape[0], node), BF16),
            pltpu.VMEM((mix.shape[0], node), BF16),
            pltpu.VMEM((couple.shape[0], node), BF16),
            pltpu.VMEM((mix.shape[0], node), BF16),
            pltpu.VMEM((couple.shape[0], node), BF16),
            pltpu.VMEM((levels, columns, node), BF16),
            pltpu.VMEM((levels, columns, node), BF16),
            pltpu.VMEM((levels, columns, node), BF16),
            pltpu.VMEM((2, columns, node), BF16),
            dma,
            dma((3, cells)),
            dma((1 + CHUNKS + 2,)),
            dma((4, CHUNKS)),
            dma((4, CHUNKS)),
            dma((pieces,)), dma((pieces,)), dma((pieces,)),
            dma((pieces,)), dma((pieces,)), dma((pieces,)),
            dma((3,)), dma((3,)),
            dma((2 * levels,)),
            dma((2 * levels,)),
            dma((2, PIECES)),
            dma((2, PIECES)),
        ],
        compiler_params=pltpu.CompilerParams(
            collective_id=0, has_side_effects=True, vmem_limit_bytes=60 * 2**20
        ),
    )(target, rhs, inverse, leaf_couple, skel, lift, mix, couple)


def hand_out_kernel(cuts, *refs):
    count = len(cuts)
    sems = refs[-1]
    inward, outward = [], []
    for src, dst, stage, cut in zip(refs[:count], refs[count : 2 * count], refs[2 * count : 3 * count], cuts):
        rows = src.shape[0] // cut
        for i in range(cut):
            part, at = pl.ds(i * rows, rows), len(inward)
            inward.append(pltpu.make_async_copy(src.at[part], stage.at[part], sems.at[0, at]))
            outward.append(pltpu.make_async_copy(stage.at[part], dst.at[part], sems.at[1, at]))
    for copy in inward:
        copy.start()
    for copy, after in zip(inward, outward):
        copy.wait()
        after.start()
    for copy in outward:
        copy.wait()


def hand_out(*arrays):
    cuts = (2, 8, 1, 1)
    hbm = pl.BlockSpec(memory_space=pl.ANY)
    return pl.pallas_call(
        functools.partial(hand_out_kernel, cuts),
        out_shape=[jax.ShapeDtypeStruct(a.shape, a.dtype) for a in arrays],
        in_specs=[hbm] * len(arrays),
        out_specs=[hbm] * len(arrays),
        scratch_shapes=[pltpu.VMEM(a.shape, a.dtype) for a in arrays]
        + [pltpu.SemaphoreType.DMA((2, sum(cuts)))],
        compiler_params=pltpu.CompilerParams(vmem_limit_bytes=60 * 2**20),
    )(*arrays)


def on_device(
    right_side, leaf_inverse, leaf_couple, skel_target, skeleton_in, lift_ops, node_mix, node_couple
):
    n = lax.axis_size("cells")
    columns, blocks, width = skeleton_in.shape
    solved, skel, node_solution, node_skeleton = hand_out(
        *tree_call(
            n, blocks, skel_target, right_side, leaf_inverse, leaf_couple,
            skeleton_in.reshape(columns * blocks, width), lift_ops[0], node_mix[0], node_couple[0],
        )
    )
    return (
        solved,
        skel.reshape(columns, blocks, width),
        node_solution[None],
        node_skeleton[None],
    )


def solution(mesh):
    return jax.shard_map(
        on_device,
        mesh=mesh,
        in_specs=(
            P("cells", "rhs", None),
            P("cells", None, None),
            P("cells", None, None, None),
            P("cells", None),
            P("rhs", "cells", None),
            P("cells", None, "rhs"),
            P("cells", None, "rhs"),
            P("cells", None, "rhs"),
        ),
        out_specs=(
            P("cells", "rhs", None),
            P("rhs", "cells", None),
            P("cells", "rhs", None),
            P("cells", "rhs", None),
        ),
        check_vma=False,
    )
```

```python
import functools

import jax
import jax.numpy as jnp
from jax import lax
from jax.experimental import pallas as pl
from jax.experimental.pallas import tpu as pltpu
from jax.sharding import PartitionSpec as P

HOP = 2
CHUNKS = 4
PARTS = 2
MESH = pl.DeviceIdType.MESH
F32, BF16 = jnp.float32, jnp.bfloat16


def dot(a, b):
    return jnp.dot(a, b, preferred_element_type=F32)


def tree_kernel(
    n, levels, target, rhs, inverse, leaf_couple, skel, lift, mix, couple,
    out_leaf, out_skel, out_sol, out_node,
    table_v, table, rhs_v, inverse_v, leaf_couple_v, leaf_v, partial, send, recv, relay, own_v, skel_v, flat, lift_g, mix_g, couple_g, mix_h, couple_h,
    mine, left_v, right_v,
    table_sem, leaf_sem, local_sem, port_send, port_recv, near_send, near_recv, far_send, far_recv, fwd_send, fwd_recv,
    half_send, half_recv, vec_send, vec_recv,
):
    me = lax.axis_index("cells")
    rank = lax.axis_index("rhs")
    near = rank + 1 - 2 * (rank % 2)
    far = (rank + 2) % 4
    far_near = (near + 2) % 4
    blocks, columns, width = own_v.shape
    node = couple_g.shape[0]
    reach = [max(1, 2 ** (level - 2)) for level in range(1, levels + 1)]
    partners = sorted({s % n for d in reach + [1, 2, n // 2] for s in (d, -d)})
    odd = me % 2
    side = 2 * odd - 1
    beside = me - side
    ahead, behind = me + 2 * side, me - 2 * side
    has_ahead = jnp.logical_and(ahead >= 0, ahead < n)
    has_behind = jnp.logical_and(behind >= 0, behind < n)
    ahead, behind = (ahead + n) % n, (behind + n) % n

    DIAG, BESIDE, AHEAD, BEHIND = range(4)
    row_of = (HOP + side, HOP - side, HOP + 2 * side, HOP - 2 * side)

    cells, slots = leaf_couple.shape[0], leaf_couple.shape[1]

    def leaf_copy(c, which):
        src, dst = ((rhs, rhs_v), (inverse, inverse_v), (leaf_couple, leaf_couple_v))[which]
        return pltpu.make_async_copy(src.at[c], dst.at[c], leaf_sem.at[which, c])

    for c in range(cells):
        for which in range(2):
            leaf_copy(c, which).start()
    for c in range(cells):
        leaf_copy(c, 2).start()

    total = cells * slots
    lanes = table_v.shape[1]
    lane = lax.broadcasted_iota(jnp.int32, (1, lanes), 1)
    block = lane + (me - HOP) * blocks
    names = [target[i // slots, i % slots] for i in range(total)]
    named = jnp.full((1, lanes), -1, jnp.int32)
    for i in range(total):
        named = jnp.where(lane == i, names[i], named)
    before = last = jnp.full((1, lanes), total, jnp.int32)
    for i in range(total):
        before = jnp.where(jnp.logical_and(named == names[i], lane > i), i, before)
        last = jnp.where(block == names[i], i, last)
    table_v[...] = jnp.zeros(table_v.shape, jnp.int32)
    table_v[0:1, :] = before
    table_v[1:2, :] = last
    table_copy = pltpu.make_async_copy(table_v, table, table_sem)
    table_copy.start()

    barrier = pltpu.get_barrier_semaphore()
    for step in partners:
        pl.semaphore_signal(barrier, inc=1, device_id=((me + step) % n, rank), device_id_type=MESH)
    for other in (near, far):
        pl.semaphore_signal(barrier, inc=1, device_id=(me, other), device_id_type=MESH)
    pl.semaphore_wait(barrier, len(partners) + 2)

    def shard(which):
        return pl.ds(pl.multiple_of(which * width, width), width)

    def remote(src, dst, s_sem, r_sem, cell, at):
        return pltpu.make_async_remote_copy(
            src_ref=src, dst_ref=dst, send_sem=s_sem, recv_sem=r_sem,
            device_id=(cell, at), device_id_type=MESH,
        )

    group = blocks // CHUNKS
    depth = lift.shape[0] // CHUNKS
    pieces = [(lift, lift_g, pl.ds(q * depth, depth)) for q in range(CHUNKS)]
    pieces += [(mix, mix_g, pl.ds(0, mix.shape[0])), (couple, couple_g, pl.ds(0, node))]
    count = len(pieces)
    halves = [(mix, mix_h, pl.ds(0, node)), (mix, mix_h, pl.ds(node, node)), (couple, couple_h, pl.ds(0, node))]

    def place(i, which):
        _, dst, rows = (pieces + halves)[i]
        return dst.at[rows, shard(which)]

    def source(i):
        return pieces[i][0].at[pieces[i][2]] if i < count else place(i, rank)

    def to_near(i):
        return remote(source(i), place(i, rank), near_send.at[i], near_recv.at[i], me, near)

    def to_far(i):
        return remote(source(i), place(i, rank), far_send.at[i], far_recv.at[i], me, far)

    def forward(i):
        return remote(place(i, far), place(i, far), fwd_send.at[i], fwd_recv.at[i], me, near)

    def near_arrival(i):
        return remote(place(i, near), place(i, near), near_send.at[i], near_recv.at[i], me, near)

    def far_arrival(i):
        return remote(place(i, far), place(i, far), far_send.at[i], far_recv.at[i], me, far)

    def fwd_arrival(i):
        return remote(place(i, far_near), place(i, far_near), fwd_send.at[i], fwd_recv.at[i], me, near)

    def across(i):
        src, dst, rows = halves[i]
        return remote(
            src.at[rows], dst.at[rows, shard(rank)], half_send.at[i], half_recv.at[i],
            (me + n // 2) % n, rank,
        )

    first_half = CHUNKS // 2

    def rows_of(q):
        return pl.ds(q * group, group)

    def rows_in_half(q):
        return pl.ds((q % first_half) * group, group)

    def diag(q):
        at = 0 if q < first_half else 1
        return remote(
            send.at[DIAG, rows_of(q)], relay.at[at, rows_in_half(q)],
            port_send.at[0, q], port_recv.at[0, q], beside if at == 0 else ahead, rank,
        )

    def to_beside(q):
        return remote(send.at[BESIDE, rows_of(q)], recv.at[0, rows_of(q)], port_send.at[1, q], port_recv.at[1, q], beside, rank)

    def to_ahead(q):
        return remote(
            send.at[AHEAD, rows_of(q)], recv.at[1, rows_of(q)],
            port_send.at[2, q], port_recv.at[2, q], ahead, rank,
        )

    def to_behind(q):
        return remote(send.at[BEHIND, rows_of(q)], recv.at[2, rows_of(q)], port_send.at[3, q], port_recv.at[3, q], behind, rank)

    for i in range(2):
        across(i).start()
    for i in range(count):
        to_far(i).start()
    for i in range(count):
        to_near(i).start()
    locals_ = [pltpu.make_async_copy(skel, skel_v, local_sem.at[0])]
    for i, (src, dst, rows) in enumerate(pieces):
        locals_.append(pltpu.make_async_copy(src.at[rows], dst.at[rows, shard(rank)], local_sem.at[1 + i]))
    for copy in locals_:
        copy.start()

    @pl.loop(0, partial.shape[0])
    def _(i):
        partial[i] = jnp.zeros((columns, width), F32)

    table_copy.wait()

    @pl.loop(0, cells)
    def _(c):
        for which in range(2):
            leaf_copy(c, which).wait()
        leaf_v[c] = dot(rhs_v[c], inverse_v[c]).astype(BF16)

    @pl.loop(0, cells)
    def _(c):
        leaf_copy(c, 2).wait()
        solved = leaf_v[c]
        for k in range(0, slots, 2):
            pair = [j for j in (k, k + 1) if j < slots]
            update = dot(solved, jnp.concatenate([leaf_couple_v[c, j] for j in pair], axis=1))
            for at, j in enumerate(pair):
                i = c * slots + j
                partial[i] = update[:, at * width : (at + 1) * width] + partial[table[0, i]]

    def emit(role, q):
        @pl.loop(q * group, (q + 1) * group)
        def _(b):
            send[role, b] = partial[table[1, row_of[role] * blocks + b]].astype(BF16)

    for at in range(first_half):
        for q in (at, at + first_half):
            emit(DIAG, q)

            @pl.when(has_ahead)
            def _():
                diag(q).start()

        emit(BEHIND, at + first_half)

        @pl.when(has_behind)
        def _():
            to_behind(at + first_half).start()

    for q in range(CHUNKS):
        if q < first_half:
            emit(BESIDE, q)
            to_beside(q).start()
        emit(AHEAD, q)

        @pl.when(has_ahead)
        def _():
            to_ahead(q).start()

    leaf_out = pltpu.make_async_copy(leaf_v, out_leaf, leaf_sem.at[0, 0])
    leaf_out.start()
    for q in range(first_half):
        emit(BEHIND, q)
        emit(BESIDE, q + first_half)

    for slot, there in ((1, has_behind), (2, has_ahead)):
        @pl.when(jnp.logical_not(there))
        def _():
            @pl.loop(0, blocks)
            def _(b):
                recv[slot, b] = jnp.zeros((columns, width), BF16)

    for copy in locals_:
        copy.wait()
    for b in range(blocks):
        own_v[b] = skel_v[pl.ds(b, columns, stride=blocks), :] - partial[table[1, HOP * blocks + b]]

    for at in range(2):
        role = (BEHIND, BESIDE)[at]
        for q in range(at * first_half, (at + 1) * first_half):
            @pl.when(has_behind)
            def _():
                diag(q).wait_recv()

                @pl.loop(q * group, (q + 1) * group)
                def _(b):
                    passing = relay[at, b - at * (blocks // 2)].astype(F32)
                    send[role, b] = (send[role, b].astype(F32) + passing).astype(BF16)

                if at == 0:
                    to_behind(q).start()

            if at == 1:
                to_beside(q).start()
        far_arrival(at).wait_recv()
        forward(at).start()

    def pass_on(i):
        across(i).wait_recv()
        to_far(count + i).start()
        to_near(count + i).start()

    total = None
    for q in range(CHUNKS):
        for i in ([], [2], [3], list(range(CHUNKS, count)))[q]:
            far_arrival(i).wait_recv()
            forward(i).start()
        if q == 1:
            for i in range(2):
                pass_on(i)
        to_beside(q).wait_recv()

        @pl.when(has_behind)
        def _():
            to_ahead(q).wait_recv()

        @pl.when(has_ahead)
        def _():
            to_behind(q).wait_recv()

        if q == CHUNKS - 1:
            across(2).start()
        for b in range(q * group, (q + 1) * group):
            arrived = recv[0, b].astype(F32) + recv[1, b].astype(F32) + recv[2, b].astype(F32)
            value = own_v[b] - arrived
            if q < CHUNKS - 1:
                skel_v[pl.ds(b, columns, stride=blocks), :] = value
            else:
                own_v[b] = value
            flat[:, b * width : (b + 1) * width] = value.astype(BF16)
        near_arrival(q).wait_recv()
        fwd_arrival(q).wait_recv()
        part = dot(flat[:, q * depth : (q + 1) * depth], lift_g[q * depth : (q + 1) * depth, :])
        total = part if total is None else total + part
    mine[0] = total.astype(BF16)

    rows = columns // PARTS
    parts = [pl.ds(h * rows, rows) for h in range(PARTS)]

    def send_up(level, h):
        return remote(
            mine.at[level, parts[h]], left_v.at[level, parts[h]], vec_send.at[2 * level, h],
            vec_recv.at[2 * level, h], (me + reach[level]) % n, rank,
        )

    def send_down(level, h):
        return remote(
            mine.at[level, parts[h]], right_v.at[level, parts[h]], vec_send.at[2 * level + 1, h],
            vec_recv.at[2 * level + 1, h], (me - reach[level] + n) % n, rank,
        )

    result = pltpu.make_async_copy(skel_v, out_skel, local_sem.at[0])

    def merge(first, second, mixing, coupling, mixed=None):
        if mixed is None:
            mixed = dot(second, mixing[node:, :])
        solved = (dot(first, mixing[:node, :]) + mixed).astype(BF16)
        skeleton = 0.5 * (first.astype(F32) + second.astype(F32)) - dot(solved, coupling[...])
        return solved, skeleton

    def next_to(level, h, skeleton):
        mine[level + 1, parts[h]] = skeleton.astype(BF16)
        send_up(level + 1, h).start()
        send_down(level + 1, h).start()

    for h in range(PARTS):
        send_up(0, h).start()
    for b in range((CHUNKS - 1) * group, blocks):
        skel_v[pl.ds(b, columns, stride=blocks), :] = own_v[b]
    result.start()
    for i in range(CHUNKS, count):
        near_arrival(i).wait_recv()
        fwd_arrival(i).wait_recv()
    mixed = dot(mine[0], mix_g[node:, :])
    for i in range(count, count + 2):
        far_arrival(i).wait_recv()
        forward(i).start()
    for h in range(PARTS):
        send_up(0, h).wait_recv()
        part = mixed[h * rows : (h + 1) * rows]
        next_to(0, h, merge(left_v[0, parts[h]], mine[0, parts[h]], mix_g, couple_g, part)[1])
    pass_on(2)

    for level in range(1, levels - 1):
        for h in range(PARTS):
            send_down(level, h).wait_recv()
            send_up(level, h).wait_recv()
            next_to(level, h, merge(left_v[level, parts[h]], right_v[level, parts[h]], mix_g, couple_g)[1])

    last = levels - 1
    far_arrival(count + 2).wait_recv()
    forward(count + 2).start()
    for i in range(count, count + len(halves)):
        near_arrival(i).wait_recv()
        fwd_arrival(i).wait_recv()
    for h in range(PARTS):
        send_down(last, h).wait_recv()
        send_up(last, h).wait_recv()
        solved, skeleton = merge(right_v[last, parts[h]], left_v[last, parts[h]], mix_h, couple_h)
        solved, skeleton = merge(skeleton.astype(BF16), solved, mix_g, couple_g)
        out_sol[parts[h], :] = solved
        out_node[parts[h], :] = skeleton

    for level in range(levels):
        for h in range(PARTS):
            send_up(level, h).wait_send()
            if level > 0:
                send_down(level, h).wait_send()
    for i in range(count + len(halves)):
        to_near(i).wait_send()
        to_far(i).wait_send()
        forward(i).wait_send()
    for i in range(len(halves)):
        across(i).wait_send()
    for q in range(CHUNKS):
        to_beside(q).wait_send()

        @pl.when(has_ahead)
        def _():
            diag(q).wait_send()
            to_ahead(q).wait_send()

        @pl.when(has_behind)
        def _():
            to_behind(q).wait_send()

    result.wait()
    leaf_out.wait()


def tree_call(n, blocks, target, rhs, inverse, leaf_couple, skel, lift, mix, couple):
    cells, columns, _ = rhs.shape
    slots, width = leaf_couple.shape[1], leaf_couple.shape[3]
    node = couple.shape[0]
    levels = n.bit_length() - 1
    pieces = CHUNKS + 2 + 3
    lanes = -(-max(cells * slots, (2 * HOP + 1) * blocks) // 128) * 128
    dma = pltpu.SemaphoreType.DMA
    vmem = pl.BlockSpec(memory_space=pltpu.VMEM)
    hbm = pl.BlockSpec(memory_space=pl.ANY)
    return pl.pallas_call(
        functools.partial(tree_kernel, n, levels),
        out_shape=[
            jax.ShapeDtypeStruct(rhs.shape, BF16),
            jax.ShapeDtypeStruct(skel.shape, F32),
            jax.ShapeDtypeStruct((columns, node), BF16),
            jax.ShapeDtypeStruct((columns, node), F32),
        ],
        in_specs=[pl.BlockSpec(memory_space=pltpu.SMEM)] + [hbm] * 7,
        out_specs=[hbm, hbm, vmem, vmem],
        scratch_shapes=[
            pltpu.VMEM((8, lanes), jnp.int32),
            pltpu.SMEM((8, lanes), jnp.int32),
            pltpu.VMEM(rhs.shape, BF16),
            pltpu.VMEM(inverse.shape, BF16),
            pltpu.VMEM(leaf_couple.shape, BF16),
            pltpu.VMEM(rhs.shape, BF16),
            pltpu.VMEM((cells * slots + 1, columns, width), F32),
            pltpu.VMEM((4, blocks, columns, width), BF16),
            pltpu.VMEM((3, blocks, columns, width), BF16),
            pltpu.VMEM((2, blocks // 2, columns, width), BF16),
            pltpu.VMEM((blocks, columns, width), F32),
            pltpu.VMEM(skel.shape, F32),
            pltpu.VMEM((columns, blocks * width), BF16),
            pltpu.VMEM((lift.shape[0], node), BF16),
            pltpu.VMEM((mix.shape[0], node), BF16),
            pltpu.VMEM((couple.shape[0], node), BF16),
            pltpu.VMEM((mix.shape[0], node), BF16),
            pltpu.VMEM((couple.shape[0], node), BF16),
            pltpu.VMEM((levels, columns, node), BF16),
            pltpu.VMEM((levels, columns, node), BF16),
            pltpu.VMEM((levels, columns, node), BF16),
            dma,
            dma((3, cells)),
            dma((1 + CHUNKS + 2,)),
            dma((4, CHUNKS)),
            dma((4, CHUNKS)),
            dma((pieces,)), dma((pieces,)), dma((pieces,)),
            dma((pieces,)), dma((pieces,)), dma((pieces,)),
            dma((3,)), dma((3,)),
            dma((2 * levels, PARTS)),
            dma((2 * levels, PARTS)),
        ],
        compiler_params=pltpu.CompilerParams(
            collective_id=0, has_side_effects=True, vmem_limit_bytes=60 * 2**20
        ),
    )(target, rhs, inverse, leaf_couple, skel, lift, mix, couple)


def hand_out_kernel(cuts, *refs):
    count = len(cuts)
    sems = refs[-1]
    inward, outward = [], []
    for src, dst, stage, cut in zip(refs[:count], refs[count : 2 * count], refs[2 * count : 3 * count], cuts):
        rows = src.shape[0] // cut
        for i in range(cut):
            part, at = pl.ds(i * rows, rows), len(inward)
            inward.append(pltpu.make_async_copy(src.at[part], stage.at[part], sems.at[0, at]))
            outward.append(pltpu.make_async_copy(stage.at[part], dst.at[part], sems.at[1, at]))
    for copy in inward:
        copy.start()
    for copy, after in zip(inward, outward):
        copy.wait()
        after.start()
    for copy in outward:
        copy.wait()


def hand_out(*arrays):
    cuts = (2, 8, 1, 1)
    hbm = pl.BlockSpec(memory_space=pl.ANY)
    return pl.pallas_call(
        functools.partial(hand_out_kernel, cuts),
        out_shape=[jax.ShapeDtypeStruct(a.shape, a.dtype) for a in arrays],
        in_specs=[hbm] * len(arrays),
        out_specs=[hbm] * len(arrays),
        scratch_shapes=[pltpu.VMEM(a.shape, a.dtype) for a in arrays]
        + [pltpu.SemaphoreType.DMA((2, sum(cuts)))],
        compiler_params=pltpu.CompilerParams(vmem_limit_bytes=60 * 2**20),
    )(*arrays)


def on_device(
    right_side, leaf_inverse, leaf_couple, skel_target, skeleton_in, lift_ops, node_mix, node_couple
):
    n = lax.axis_size("cells")
    columns, blocks, width = skeleton_in.shape
    solved, skel, node_solution, node_skeleton = hand_out(
        *tree_call(
            n, blocks, skel_target, right_side, leaf_inverse, leaf_couple,
            skeleton_in.reshape(columns * blocks, width), lift_ops[0], node_mix[0], node_couple[0],
        )
    )
    return (
        solved,
        skel.reshape(columns, blocks, width),
        node_solution[None],
        node_skeleton[None],
    )


def solution(mesh):
    return jax.shard_map(
        on_device,
        mesh=mesh,
        in_specs=(
            P("cells", "rhs", None),
            P("cells", None, None),
            P("cells", None, None, None),
            P("cells", None),
            P("rhs", "cells", None),
            P("cells", None, "rhs"),
            P("cells", None, "rhs"),
            P("cells", None, "rhs"),
        ),
        out_specs=(
            P("cells", "rhs", None),
            P("rhs", "cells", None),
            P("cells", "rhs", None),
            P("cells", "rhs", None),
        ),
        check_vma=False,
    )
```
